128 devices in a mesh: row: 16 (over x, z_hi, core), col: 8 (over z_lo, y).
Axes of the slice: x: 4, y: 4, z: 4 (z_hi: 2, z_lo: 2; z = z_hi * 2 + z_lo), core: 2. Of those that a mesh axis runs over, the one named last changes fastest.
Arguments:
- base_weights: bfloat16 [2, 8192, 28672], P(None, 'row', 'col'), may hold values from -6 to 6
- left_factors: bfloat16 [2, 8192, 8, 128], P(None, 'row', 'col'), may hold values from -6 to 6
- right_factors: bfloat16 [2, 8, 128, 28672], P(None, 'col', None, 'row'), may hold values from -6 to 6
- client_adapter_ranks: int32 [8], replicated, may hold values from 16 to 128, as said below
- step_counts: int32 [8], replicated, may hold values from 100 to 1000
- worker_slot: int32 [8], replicated, may hold values from 0 to 7, each once
Outputs:
- merged: bfloat16 [2, 8192, 28672], P(None, 'row', 'col')
The draws below stay inside these ranges and needn't reach their ends.
Inputs may be any that keep to these rules, and one draw needn't show every extreme that they name: `client_adapter_ranks`: each rank is a multiple of 16; the ranks sum to 512; at least one rank equals 128. `worker_slot`: a permutation: every slot holds exactly one worker's factors.
All inputs are finite; a program needn't handle non-finite values.
Results may differ from the reference program's by a relative error of at most 0.0045.
Values may be sent and summed in bfloat16 or wider, within the bound.
A program may use at most 128 MiB of HBM per device.

```python
import jax
import jax.numpy as jnp
from jax import lax

D = 8192
FF = 28672
RMAX = 128
PROJ = 2
ADAPTER_ALPHA = 32
CLIENT_COUNT = 8
RANKS = 512


def draw_client_adapter_ranks(key, part):
    key_big, key_fill = jax.random.split(jax.random.fold_in(key, 17))
    worker_ids = jnp.arange(CLIENT_COUNT, dtype=jnp.int32)
    big_slot = jax.random.randint(key_big, (), 0, CLIENT_COUNT)
    rank_units = jnp.where(worker_ids == big_slot, 8, 1).astype(jnp.int32)
    fill_keys = jax.random.split(key_fill, 3 * CLIENT_COUNT - 7)

    def increment_unit(current, subkey):
        scores = jax.random.randint(subkey, (CLIENT_COUNT,), 0, 1 << 20) * CLIENT_COUNT + worker_ids
        scores = jnp.where(current < 8, scores, -1)
        selected_rank = jnp.argmax(scores)
        return (current + (worker_ids == selected_rank).astype(jnp.int32), None)
    rank_units, unused = lax.scan(increment_unit, rank_units, fill_keys)
    return (rank_units * (RMAX // 8)).astype(jnp.int32)


def plant(values, rng, smallest, largest):
    index_at = [jax.random.randint(jax.random.fold_in(rng, axis), (), 0, length) for axis, length in enumerate(values.shape)]
    widest = values.shape.index(max(values.shape))
    next_to = index_at[:widest] + [(index_at[widest] + 1) % values.shape[widest]] + index_at[widest + 1:]
    return values.at[tuple(index_at)].set(smallest).at[tuple(next_to)].set(largest)


def block_scale(stream_key, dims, shards, least, high):
    def one(dim, blocks):
        steps = jax.random.uniform(jax.random.fold_in(jax.random.fold_in(stream_key, 6), dim), (blocks,), jnp.float32, least / len(shards), high / len(shards))
        return jnp.repeat(jnp.exp(steps), dims[dim] // blocks).reshape((-1,) + (1,) * (len(dims) - dim - 1))

    gain = one(*shards[0])
    for cut in shards[1:]:
        gain = gain * one(*cut)
    return gain


def scatter_about(key, extent, scale, reach, pieces=(), kind=jnp.bfloat16):
    drawn = jax.random.normal(key, extent, jnp.float32) * scale
    if len(pieces) > 0:
        drawn = block_scale(key, extent, pieces, -0.22, 0.18) * drawn
    return jnp.clip(drawn, min=-reach, max=reach).astype(kind)


def setup_inputs(seed: int = 0) -> dict:
    key_of = jax.random.split(jax.random.key(seed), 7)
    return {
        "base_weights": scatter_about(key_of[0], (PROJ, D, FF), 1.0, 6.0, ((1, 16), (2, 8))),
        "left_factors": scatter_about(key_of[1], (PROJ, D, CLIENT_COUNT, RMAX), 1.0, 6.0, ((1, 16), (2, 8))),
        "right_factors": scatter_about(key_of[2], (PROJ, CLIENT_COUNT, RMAX, FF), 1.0, 6.0, ((1, 8), (3, 16))),
        "client_adapter_ranks": draw_client_adapter_ranks(jax.random.fold_in(key_of[6], 71), 0),
        "step_counts": plant(jax.random.randint(key_of[4], (CLIENT_COUNT,), 100, 1001), jax.random.fold_in(key_of[4], 1), 100, 1000).astype(jnp.int32),
        "worker_slot": jax.random.permutation(key_of[5], CLIENT_COUNT).astype(jnp.int32),
    }


def slot_tables(client_adapter_ranks, step_counts, worker_slot):
    slot_ids = jnp.arange(CLIENT_COUNT, dtype=jnp.int32)
    slot_hot = worker_slot[:, None] == slot_ids[None, :]
    rank_slot = jnp.sum(jnp.where(slot_hot, client_adapter_ranks[:, None], 0), axis=0).astype(jnp.int32)
    counts = step_counts.astype(jnp.float32)
    per_step_portion = counts / jnp.sum(counts)
    client_scale = ADAPTER_ALPHA * per_step_portion / client_adapter_ranks.astype(jnp.float32)
    slot_scale_factor = jnp.sum(jnp.where(slot_hot, client_scale[:, None], 0.0), axis=0)
    return rank_slot, slot_scale_factor


def packed_index(rank_slot, rank_cap, total):
    workers = rank_slot.shape[0]
    slot_ends = jnp.cumsum(rank_slot).astype(jnp.int32)
    slot_starts = slot_ends - rank_slot
    position = jnp.arange(total, dtype=jnp.int32)
    slot_of = jnp.sum((position[:, None] >= slot_ends[None, :]).astype(jnp.int32), axis=1)
    slot_ids = jnp.arange(workers, dtype=jnp.int32)
    start_of = jnp.sum(jnp.where(slot_of[:, None] == slot_ids[None, :], slot_starts[None, :], 0), axis=1)
    return (slot_of * rank_cap + position - start_of).astype(jnp.int32)


def reference(base_weights, left_factors, right_factors, client_adapter_ranks, step_counts, worker_slot):
    rank_slot, slot_scale_factor = slot_tables(client_adapter_ranks, step_counts, worker_slot)
    columns = jnp.arange(RMAX, dtype=jnp.int32)
    rank_scale = jnp.where(columns[None, :] < rank_slot[:, None], slot_scale_factor[:, None], 0.0)
    scaled_right = (right_factors.astype(jnp.float32) * rank_scale[None, :, :, None]).astype(jnp.bfloat16)
    flat_index = packed_index(rank_slot, RMAX, RANKS)

    def merge_one(operands):
        base_tile, left_block, right_block = operands
        left_pack = jnp.take(left_block.reshape(D, CLIENT_COUNT * RMAX), flat_index, axis=1)
        right_pack = jnp.take(right_block.reshape(CLIENT_COUNT * RMAX, FF), flat_index, axis=0)
        delta_tile = jnp.dot(left_pack.astype(jnp.float32), right_pack.astype(jnp.float32), preferred_element_type=jnp.float32)
        return (base_tile.astype(jnp.float32) + delta_tile).astype(jnp.bfloat16)

    return lax.map(merge_one, (base_weights, left_factors, scaled_right))
```

```python
import functools

import jax
import jax.numpy as jnp
from jax import lax
from jax.experimental import pallas as pl
from jax.experimental.pallas import tpu as pltpu
from jax.sharding import PartitionSpec as P

ADAPTER_ALPHA = 32
MESH = pl.DeviceIdType.MESH
BF16 = jnp.bfloat16
F32 = jnp.float32
SLOTS = 8
UNIT = 16
ROUTE1_TILES = 9


def slot_ends(ranks, slots):
    ends, total = [], jnp.int32(0)
    for s in range(SLOTS):
        for w in range(SLOTS):
            total = total + jnp.where(slots[w] == s, ranks[w], 0)
        ends.append(total // UNIT)
    return ends


def slot_and_start(position, ends):
    slot = jnp.zeros_like(position)
    start = jnp.zeros_like(position)
    for s in range(SLOTS - 1):
        past = position >= ends[s]
        slot = slot + jnp.where(past, 1, 0)
        start = jnp.where(past, ends[s], start)
    return slot, start


class Copies:
    def __init__(self, send_sems, recv_sems):
        self.send_sems, self.recv_sems = send_sems, recv_sems
        self.count, self.started = 0, []

    def start(self, src, dst, event, device):
        copy = pltpu.make_async_remote_copy(
            src_ref=src,
            dst_ref=dst,
            send_sem=self.send_sems.at[self.count],
            recv_sem=self.recv_sems.at[event],
            device_id=device,
            device_id_type=MESH,
        )
        self.count += 1
        copy.start()
        self.started.append((copy, None))

    def start_or_local(self, src, dst, event, device, local):
        copy = pltpu.make_async_remote_copy(
            src_ref=src,
            dst_ref=dst,
            send_sem=self.send_sems.at[self.count],
            recv_sem=self.recv_sems.at[event],
            device_id=device,
            device_id_type=MESH,
        )
        own = pltpu.make_async_copy(src, dst, self.recv_sems.at[event])
        self.count += 1
        remote = jnp.logical_not(local)
        pl.when(remote)(copy.start)
        pl.when(local)(own.start)
        self.started.append((copy, remote))

    def arrived(self, dst, event, device):
        pltpu.make_async_remote_copy(
            src_ref=dst,
            dst_ref=dst,
            send_sem=self.send_sems.at[0],
            recv_sem=self.recv_sems.at[event],
            device_id=device,
            device_id_type=MESH,
        ).wait_recv()

    def finish(self):
        for copy, when in self.started:
            if when is None:
                copy.wait_send()
            else:
                pl.when(when)(copy.wait_send)


N_A1, N_A2, N_L, N_B = 16, 8, 9, 17 + 16
N_RECV = N_A1 + N_A2 + N_L + 2 * N_B
N_SEND = 16 + 6 + 9 + 2 * 33


def gather_kernel(
    ranks, steps, slots, left, right, r1, r2, packed_left, staged, first, second0, second1, lefts, send_sems, recv_sems
):
    row, col = lax.axis_index("row"), lax.axis_index("col")
    x, zh, core = row // 4, (row // 2) % 2, row % 2
    zl, y = col // 4, col % 4
    t = row // 2

    def dev(x_=x, zh_=zh, core_=core, y_=y, zl_=zl):
        return (x_ * 4 + zh_ * 2 + core_, zl_ * 4 + y_)

    xr, xl, xo = (x + 1) % 4, (x + 3) % 4, (x + 2) % 4
    yr, yl, yo = (y + 1) % 4, (y + 3) % 4, (y + 2) % 4
    zo, co, zlo = 1 - zh, 1 - core, 1 - zl
    right_x, left_x = dev(x_=xr), dev(x_=xl)
    right_y, left_y = dev(y_=yr), dev(y_=yl)
    over_z, sibling, over_zl = dev(zh_=zo), dev(core_=co), dev(zl_=zlo)

    barrier = pltpu.get_barrier_semaphore()
    greeted = [right_x, left_x, over_z, sibling, over_zl, right_y, left_y, dev(y_=yo)]
    for a in range(2):
        for zh0 in range(2):
            for zl0 in range(2):
                greeted.append(dev(x_=2 * zl + a, zh_=zh0, zl_=zl0))
    for device in greeted:
        pl.semaphore_signal(barrier, inc=1, device_id=device, device_id_type=MESH)
    pl.semaphore_wait(barrier, len(greeted))

    copies = Copies(send_sems, recv_sems)
    second = (second0, second1)

    ends = slot_ends(ranks, slots)
    own_rank, own_steps, all_steps = jnp.int32(0), jnp.int32(0), jnp.int32(0)
    for w in range(SLOTS):
        mine = slots[w] == col
        own_rank = own_rank + jnp.where(mine, ranks[w], 0)
        own_steps = own_steps + jnp.where(mine, steps[w], 0)
        all_steps = all_steps + steps[w]
    own_start = jnp.int32(0)
    for s in range(SLOTS - 1):
        own_start = jnp.where(col == s + 1, ends[s], own_start)

    def as_vector(v):
        return jnp.full((1, 128), v, jnp.int32).astype(F32)

    scale = ADAPTER_ALPHA * (as_vector(own_steps) / as_vector(all_steps)) / as_vector(own_rank)
    scale = jnp.concatenate([scale] * (right.shape[3] // 128), axis=1)

    ystar, zlstar = 2 * (x % 2) + zh, x // 2

    def a1_event(p, ystar_, zl_):
        return (p * 4 + ystar_) * 2 + zl_

    for p in range(2):
        for dz in range(2):
            for dx in (2, 1, 3, 0):
                x2, zh2 = (x + dx) % 4, (zh + dz) % 2
                t2 = x2 * 2 + zh2
                k = jnp.bitwise_and(t2 - own_start + 64, 7)
                staged[p, t2] = (right[p, k].astype(F32) * scale).astype(BF16)
                src, dst = staged.at[p, t2], first.at[p, ystar, zl]
                event, device = a1_event(p, ystar, zl), dev(x_=x2, zh_=zh2, zl_=zlstar)
                if dx == 0 and dz == 0:
                    copies.start_or_local(src, dst, event, device, zl == zlstar)
                else:
                    copies.start(src, dst, event, device)
        if p == 0:
            L0 = N_A1 + N_A2
            copies.start(left, lefts.at[col], L0 + 0, right_y)
            copies.start(left, lefts.at[col], L0 + 1, left_y)

    lefts[col] = left[...]

    def a2_event(p, y_):
        return N_A1 + p * 4 + y_

    for p in range(2):
        for dy in (2, 1, 3, 0):
            y2 = (y + dy) % 4
            for zl0 in range(2):
                copies.arrived(first.at[p, y2, zl0], a1_event(p, y2, zl0), sibling)
            if dy:
                copies.start(first.at[p, y2], second[p].at[y], a2_event(p, y), dev(y_=y2))
            else:
                second[p][y] = first[p, y]

    copies.start(left, lefts.at[col], L0 + 2, over_zl)

    def col_of(y_, zl_):
        return zl_ * 4 + y_

    def pass_left(base, zl_):
        c_from_left, c_from_right = col_of(yl, zl_), col_of(yr, zl_)
        copies.arrived(lefts.at[c_from_left], L0 + base, sibling)
        copies.start(lefts.at[c_from_left, 0], lefts.at[c_from_left, 0], L0 + base + 3, right_y)
        copies.arrived(lefts.at[c_from_right], L0 + base + 1, sibling)
        copies.start(lefts.at[c_from_right, 1], lefts.at[c_from_right, 1], L0 + base + 4, left_y)

    pass_left(0, zl)

    BLK = [t, xl * 2 + zh, xr * 2 + zh, xo * 2 + zh, x * 2 + zo, xl * 2 + zo, xr * 2 + zo, xo * 2 + zo]
    HALF = [pl.ds(0, 32), pl.ds(32, 32)]

    def b_event(p, n):
        return N_A1 + N_A2 + N_L + p * N_B + n

    def at(ref, p, blk, rows=None, half=core):
        return ref.at[half, blk, p] if rows is None else ref.at[half, blk, p, rows]

    def go(ref, p, blk, n, device, rows=None):
        copies.start(at(ref, p, blk, rows), at(ref, p, blk, rows), b_event(p, n), device)

    def got(ref, p, blk, n, rows=None, half=core):
        copies.arrived(at(ref, p, blk, rows, half), b_event(p, n), sibling)

    def share(p, route, i):
        go((r1, r2)[route], p, BLK[i], 17 + route * 8 + i, sibling)

    def pack(p):
        for y0 in (1, 2, 3):
            y2 = (y + y0) % 4
            copies.arrived(second[p].at[y2], a2_event(p, y2), sibling)
        width = r1.shape[4]
        for i in range(4):
            slot, _ = slot_and_start(t + 8 * i, ends)
            unit = second[p][jnp.bitwise_and(slot, 3), jnp.right_shift(slot, 2)]
            r1[core, t, p, pl.ds(UNIT * i, UNIT)] = unit[:, :width]
            r2[core, t, p, pl.ds(UNIT * i, UNIT)] = unit[:, width:]
        go(r2, p, t, 0, right_x)
        go(r2, p, t, 1, left_x)
        go(r1, p, t, 8, over_z)
        go(r1, p, t, 9, right_x)
        go(r1, p, t, 10, left_x)
        go(r2, p, t, 4, over_z)
        share(p, 0, 0)
        share(p, 1, 0)

    def early(p):
        got(r2, p, BLK[1], 0)
        go(r2, p, BLK[1], 2, right_x, HALF[0])
        go(r2, p, BLK[1], 5, over_z)
        share(p, 1, 1)
        got(r2, p, BLK[2], 1)
        go(r2, p, BLK[2], 3, left_x, HALF[1])
        go(r2, p, BLK[2], 6, over_z)
        share(p, 1, 2)
        got(r1, p, BLK[4], 8)
        go(r1, p, BLK[4], 13, right_x)
        go(r1, p, BLK[4], 14, left_x)
        share(p, 0, 4)

    def middle(p):
        got(r1, p, BLK[1], 9)
        go(r1, p, BLK[1], 11, right_x, HALF[0])
        share(p, 0, 1)
        got(r1, p, BLK[2], 10)
        go(r1, p, BLK[2], 12, left_x, HALF[1])
        share(p, 0, 2)
        got(r2, p, BLK[3], 2, HALF[0])
        got(r2, p, BLK[3], 3, HALF[1])
        go(r2, p, BLK[3], 7, over_z)
        share(p, 1, 3)
        got(r2, p, BLK[4], 4)
        share(p, 1, 4)

    def late(p):
        got(r1, p, BLK[5], 13)
        go(r1, p, BLK[5], 15, right_x, HALF[0])
        share(p, 0, 5)
        got(r1, p, BLK[6], 14)
        go(r1, p, BLK[6], 16, left_x, HALF[1])
        share(p, 0, 6)
        got(r1, p, BLK[3], 11, HALF[0])
        got(r1, p, BLK[3], 12, HALF[1])
        share(p, 0, 3)
        got(r2, p, BLK[5], 5)
        share(p, 1, 5)
        got(r2, p, BLK[6], 6)
        share(p, 1, 6)

    def last(p):
        got(r2, p, BLK[7], 7)
        share(p, 1, 7)
        got(r1, p, BLK[7], 15, HALF[0])
        got(r1, p, BLK[7], 16, HALF[1])
        share(p, 0, 7)

    def shared(p):
        for route in range(2):
            for i in range(8):
                got((r1, r2)[route], p, BLK[i], 17 + route * 8 + i, half=co)

    pack(0)
    copies.arrived(lefts.at[col_of(y, zlo)], L0 + 2, sibling)
    other = lefts.at[col_of(y, zlo)]
    copies.start(other, other, L0 + 5, right_y)
    copies.start(other, other, L0 + 6, left_y)
    early(0)
    pack(1)
    middle(0)
    early(1)
    c_l, c_r, c_o = col_of(yl, zlo), col_of(yr, zlo), col_of(yo, zlo)
    copies.arrived(lefts.at[c_l], L0 + 5, sibling)
    copies.start(lefts.at[c_l, 0], lefts.at[c_l, 0], L0 + 7, right_y)
    copies.arrived(lefts.at[c_r], L0 + 6, sibling)
    copies.start(lefts.at[c_r, 1], lefts.at[c_r, 1], L0 + 8, left_y)
    late(0)
    middle(1)
    late(1)

    own_o = col_of(yo, zl)
    copies.arrived(lefts.at[own_o, 0], L0 + 3, sibling)
    copies.arrived(lefts.at[own_o, 1], L0 + 4, sibling)
    copies.arrived(lefts.at[c_o, 0], L0 + 7, sibling)
    copies.arrived(lefts.at[c_o, 1], L0 + 8, sibling)
    depth = packed_left.shape[2]
    lane = lax.broadcasted_iota(jnp.int32, (1, depth), 1)
    position = lane // 64 + 8 * ((lane // UNIT) % 4)
    slot, start = slot_and_start(position, ends)
    source = slot * 128 + (position - start) * UNIT + lane % UNIT
    picked = [None, None]
    for s in range(SLOTS):
        k = lax.broadcasted_iota(jnp.int32, (128, depth), 0) + s * 128
        pick = jnp.where(k == source, 1.0, 0.0).astype(BF16)
        for p in range(2):
            part = jnp.dot(lefts[s, p], pick, preferred_element_type=F32)
            picked[p] = part if picked[p] is None else picked[p] + part
    for p in range(2):
        packed_left[p] = picked[p].astype(BF16)

    last(0)
    last(1)
    shared(0)
    shared(1)
    copies.finish()


def merge_kernel(base, packed_left, r1, r2, out):
    width = r1.shape[4]
    lhs = packed_left[0]
    for ref, lo, hi in ((r1, 0, width), (r2, width, out.shape[2])):
        rhs = ref[0, :, 0].reshape(lhs.shape[1], hi - lo)
        delta = jnp.dot(lhs, rhs, preferred_element_type=F32)
        out[0, :, lo:hi] = (base[0, :, lo:hi].astype(F32) + delta).astype(BF16)


def body(base, left, right, ranks, steps, slots):
    projections, rows, columns = base.shape
    half = columns // 2
    left = left.reshape(projections, rows, 128)
    right = right.reshape(projections, 8, UNIT, half)
    w1 = ROUTE1_TILES * 128
    w2 = half - w1
    vmem = pl.BlockSpec(memory_space=pltpu.VMEM)
    smem = pl.BlockSpec(memory_space=pltpu.SMEM)
    r1, r2, packed_left = pl.pallas_call(
        gather_kernel,
        out_shape=(
            jax.ShapeDtypeStruct((2, 8, 2, 64, w1), BF16),
            jax.ShapeDtypeStruct((2, 8, 2, 64, w2), BF16),
            jax.ShapeDtypeStruct((2, rows, 512), BF16),
        ),
        in_specs=[smem, smem, smem, vmem, vmem],
        out_specs=(vmem, vmem, vmem),
        scratch_shapes=[
            pltpu.VMEM((2, 8, UNIT, half), BF16),
            pltpu.VMEM((2, 4, 2, UNIT, half), BF16),
            pltpu.VMEM((4, 2, UNIT, half), BF16),
            pltpu.VMEM((4, 2, UNIT, half), BF16),
            pltpu.VMEM((8, 2, rows, 128), BF16),
            pltpu.SemaphoreType.DMA((N_SEND,)),
            pltpu.SemaphoreType.DMA((N_RECV,)),
        ],
        compiler_params=pltpu.CompilerParams(
            collective_id=0, has_side_effects=True, vmem_limit_bytes=40 * 2**20
        ),
        name="gather_factors",
    )(ranks, steps, slots, left, right)
    return pl.pallas_call(
        merge_kernel,
        grid=(projections, 2),
        out_shape=jax.ShapeDtypeStruct(base.shape, BF16),
        in_specs=[
            pl.BlockSpec((1, rows, half), lambda p, h: (p, 0, h)),
            pl.BlockSpec((1, rows, 512), lambda p, h: (p, 0, 0)),
            pl.BlockSpec((1, 8, 1, 64, w1), lambda p, h: (h, 0, p, 0, 0)),
            pl.BlockSpec((1, 8, 1, 64, w2), lambda p, h: (h, 0, p, 0, 0)),
        ],
        out_specs=pl.BlockSpec((1, rows, half), lambda p, h: (p, 0, h)),
        compiler_params=pltpu.CompilerParams(vmem_limit_bytes=40 * 2**20),
        name="merge_blocks",
    )(base, packed_left, r1, r2)


def solution(mesh):
    placed = (P(None, "row", "col"), P(None, "row", "col", None), P(None, "col", None, "row"), P(), P(), P())
    return jax.shard_map(
        body, mesh=mesh, in_specs=placed, out_specs=P(None, "row", "col"), check_vma=False
    )
```

```python
import functools

import jax
import jax.numpy as jnp
from jax import lax
from jax.experimental import pallas as pl
from jax.experimental.pallas import tpu as pltpu
from jax.sharding import PartitionSpec as P

ADAPTER_ALPHA = 32
MESH = pl.DeviceIdType.MESH
BF16 = jnp.bfloat16
F32 = jnp.float32
SLOTS = 8
UNIT = 16
ROUTE1_TILES = 9


def slot_ends(ranks, slots):
    ends, total = [], jnp.int32(0)
    for s in range(SLOTS):
        for w in range(SLOTS):
            total = total + jnp.where(slots[w] == s, ranks[w], 0)
        ends.append(total // UNIT)
    return ends


def slot_and_start(position, ends):
    slot = jnp.zeros_like(position)
    start = jnp.zeros_like(position)
    for s in range(SLOTS - 1):
        past = position >= ends[s]
        slot = slot + jnp.where(past, 1, 0)
        start = jnp.where(past, ends[s], start)
    return slot, start


class Copies:
    def __init__(self, send_sems, recv_sems):
        self.send_sems, self.recv_sems = send_sems, recv_sems
        self.count, self.started = 0, []

    def start(self, src, dst, event, device):
        copy = pltpu.make_async_remote_copy(
            src_ref=src,
            dst_ref=dst,
            send_sem=self.send_sems.at[self.count],
            recv_sem=self.recv_sems.at[event],
            device_id=device,
            device_id_type=MESH,
        )
        self.count += 1
        copy.start()
        self.started.append((copy, None))

    def start_or_local(self, src, dst, event, device, local):
        copy = pltpu.make_async_remote_copy(
            src_ref=src,
            dst_ref=dst,
            send_sem=self.send_sems.at[self.count],
            recv_sem=self.recv_sems.at[event],
            device_id=device,
            device_id_type=MESH,
        )
        own = pltpu.make_async_copy(src, dst, self.recv_sems.at[event])
        self.count += 1
        remote = jnp.logical_not(local)
        pl.when(remote)(copy.start)
        pl.when(local)(own.start)
        self.started.append((copy, remote))

    def arrived(self, dst, event, device):
        pltpu.make_async_remote_copy(
            src_ref=dst,
            dst_ref=dst,
            send_sem=self.send_sems.at[0],
            recv_sem=self.recv_sems.at[event],
            device_id=device,
            device_id_type=MESH,
        ).wait_recv()

    def finish(self):
        for copy, when in self.started:
            if when is None:
                copy.wait_send()
            else:
                pl.when(when)(copy.wait_send)


N_A1, N_A2, N_L, N_B = 16, 8, 9, 17 + 16
N_RECV = N_A1 + N_A2 + N_L + 2 * N_B
N_SEND = 16 + 6 + 9 + 2 * 33


def gather_kernel(
    ranks_hbm,
    steps_hbm,
    slots_hbm,
    left,
    right_hbm,
    base,
    r1,
    r2,
    packed_left,
    merged,
    base_last,
    ranks,
    steps,
    slots,
    right0,
    right1,
    base_first,
    staged,
    first,
    second0,
    second1,
    lefts,
    send_sems,
    recv_sems,
    own_sems,
):
    row, col = lax.axis_index("row"), lax.axis_index("col")
    x, zh, core = row // 4, (row // 2) % 2, row % 2
    zl, y = col // 4, col % 4
    t = row // 2

    def dev(x_=x, zh_=zh, core_=core, y_=y, zl_=zl):
        return (x_ * 4 + zh_ * 2 + core_, zl_ * 4 + y_)

    xr, xl, xo = (x + 1) % 4, (x + 3) % 4, (x + 2) % 4
    yr, yl, yo = (y + 1) % 4, (y + 3) % 4, (y + 2) % 4
    zo, co, zlo = 1 - zh, 1 - core, 1 - zl
    right_x, left_x = dev(x_=xr), dev(x_=xl)
    right_y, left_y = dev(y_=yr), dev(y_=yl)
    over_z, sibling, over_zl = dev(zh_=zo), dev(core_=co), dev(zl_=zlo)

    barrier = pltpu.get_barrier_semaphore()
    greeted = [right_x, left_x, over_z, sibling, over_zl, right_y, left_y, dev(y_=yo)]
    for a in range(2):
        for zh0 in range(2):
            for zl0 in range(2):
                greeted.append(dev(x_=2 * zl + a, zh_=zh0, zl_=zl0))
    for device in greeted:
        pl.semaphore_signal(barrier, inc=1, device_id=device, device_id_type=MESH)

    copies = Copies(send_sems, recv_sems)
    second, right = (second0, second1), (right0, right1)
    pairs = (
        (ranks_hbm, ranks),
        (steps_hbm, steps),
        (slots_hbm, slots),
        (right_hbm.at[0], right[0]),
        (right_hbm.at[1], right[1]),
        (left, lefts.at[col]),
        (base.at[0], base_first),
        (base.at[1], base_last),
    )
    local = [pltpu.make_async_copy(src, dst, own_sems.at[n]) for n, (src, dst) in enumerate(pairs)]
    for copy in local[:6]:
        copy.start()
    for copy in local[:3]:
        copy.wait()

    ends = slot_ends(ranks, slots)
    own_rank, own_steps, all_steps = jnp.int32(0), jnp.int32(0), jnp.int32(0)
    for w in range(SLOTS):
        mine = slots[w] == col
        own_rank = own_rank + jnp.where(mine, ranks[w], 0)
        own_steps = own_steps + jnp.where(mine, steps[w], 0)
        all_steps = all_steps + steps[w]
    own_start = jnp.int32(0)
    for s in range(SLOTS - 1):
        own_start = jnp.where(col == s + 1, ends[s], own_start)

    def as_vector(v):
        return jnp.full((1, 128), v, jnp.int32).astype(F32)

    scale = ADAPTER_ALPHA * (as_vector(own_steps) / as_vector(all_steps)) / as_vector(own_rank)
    scale = jnp.concatenate([scale] * (right0.shape[2] // 128), axis=1)

    ystar, zlstar = 2 * (x % 2) + zh, x // 2

    def a1_event(p, ystar_, zl_):
        return (p * 4 + ystar_) * 2 + zl_

    def stage(p):
        local[3 + p].wait()
        for t2 in range(8):
            k = jnp.bitwise_and(t2 - own_start + 64, 7)
            staged[p, t2] = (right[p][k].astype(F32) * scale).astype(BF16)

    def send_units(p):
        for dz in range(2):
            for dx in (2, 1, 3, 0):
                x2, zh2 = (x + dx) % 4, (zh + dz) % 2
                src, dst = staged.at[p, x2 * 2 + zh2], first.at[p, ystar, zl]
                event, device = a1_event(p, ystar, zl), dev(x_=x2, zh_=zh2, zl_=zlstar)
                if dx == 0 and dz == 0:
                    copies.start_or_local(src, dst, event, device, zl == zlstar)
                else:
                    copies.start(src, dst, event, device)

    stage(0)
    pl.semaphore_wait(barrier, len(greeted))
    send_units(0)
    stage(1)
    send_units(1)
    L0 = N_A1 + N_A2
    own_left = lefts.at[col]
    local[5].wait()
    copies.start(own_left, own_left, L0 + 0, right_y)
    copies.start(own_left, own_left, L0 + 1, left_y)
    local[6].start()
    local[7].start()

    depth = packed_left.shape[2]
    lane = lax.broadcasted_iota(jnp.int32, (1, depth), 1)
    position = lane // 64 + 8 * ((lane // UNIT) % 4)
    lane_slot, lane_start = slot_and_start(position, ends)
    source = lane_slot * 128 + (position - lane_start) * UNIT + lane % UNIT

    def pick_left(slot, init=False):
        k = lax.broadcasted_iota(jnp.int32, (128, depth), 0) + slot * 128
        pick = jnp.where(k == source, 1.0, 0.0).astype(BF16)
        for p in range(2):
            part = jnp.dot(lefts[slot, p], pick, preferred_element_type=F32).astype(BF16)
            packed_left[p] = part if init else packed_left[p] + part

    pick_left(col, init=True)

    def a2_event(p, y_):
        return N_A1 + p * 4 + y_

    for p in range(2):
        for dy in (2, 1, 3, 0):
            y2 = (y + dy) % 4
            for zl0 in range(2):
                copies.arrived(first.at[p, y2, zl0], a1_event(p, y2, zl0), sibling)
            if dy:
                copies.start(first.at[p, y2], second[p].at[y], a2_event(p, y), dev(y_=y2))
            else:
                second[p][y] = first[p, y]

    copies.start(own_left, own_left, L0 + 2, over_zl)

    def col_of(y_, zl_):
        return zl_ * 4 + y_

    def pass_left(base, zl_):
        c_from_left, c_from_right = col_of(yl, zl_), col_of(yr, zl_)
        copies.arrived(lefts.at[c_from_left], L0 + base, sibling)
        copies.start(lefts.at[c_from_left, 0], lefts.at[c_from_left, 0], L0 + base + 3, right_y)
        copies.arrived(lefts.at[c_from_right], L0 + base + 1, sibling)
        copies.start(lefts.at[c_from_right, 1], lefts.at[c_from_right, 1], L0 + base + 4, left_y)
        pick_left(c_from_left)
        pick_left(c_from_right)

    pass_left(0, zl)

    BLK = [t, xl * 2 + zh, xr * 2 + zh, xo * 2 + zh, x * 2 + zo, xl * 2 + zo, xr * 2 + zo, xo * 2 + zo]
    HALF = [pl.ds(0, 32), pl.ds(32, 32)]

    def b_event(p, n):
        return N_A1 + N_A2 + N_L + p * N_B + n

    def at(ref, p, blk, rows=None, half=core):
        return ref.at[half, blk, p] if rows is None else ref.at[half, blk, p, rows]

    def go(ref, p, blk, n, device, rows=None):
        copies.start(at(ref, p, blk, rows), at(ref, p, blk, rows), b_event(p, n), device)

    def got(ref, p, blk, n, rows=None, half=core):
        copies.arrived(at(ref, p, blk, rows, half), b_event(p, n), sibling)

    def share(p, route, i):
        go((r1, r2)[route], p, BLK[i], 17 + route * 8 + i, sibling)

    def pack(p):
        for y0 in (1, 2, 3):
            y2 = (y + y0) % 4
            copies.arrived(second[p].at[y2], a2_event(p, y2), sibling)
        width = r1.shape[4]
        for i in range(4):
            slot, _ = slot_and_start(t + 8 * i, ends)
            unit = second[p][jnp.bitwise_and(slot, 3), jnp.right_shift(slot, 2)]
            r1[core, t, p, pl.ds(UNIT * i, UNIT)] = unit[:, :width]
            r2[core, t, p, pl.ds(UNIT * i, UNIT)] = unit[:, width:]
        go(r2, p, t, 0, right_x)
        go(r2, p, t, 1, left_x)
        go(r1, p, t, 8, over_z)
        go(r1, p, t, 9, right_x)
        go(r1, p, t, 10, left_x)
        go(r2, p, t, 4, over_z)
        share(p, 0, 0)
        share(p, 1, 0)

    def early(p):
        got(r2, p, BLK[1], 0)
        go(r2, p, BLK[1], 2, right_x, HALF[0])
        go(r2, p, BLK[1], 5, over_z)
        share(p, 1, 1)
        got(r2, p, BLK[2], 1)
        go(r2, p, BLK[2], 3, left_x, HALF[1])
        go(r2, p, BLK[2], 6, over_z)
        share(p, 1, 2)
        got(r1, p, BLK[4], 8)
        go(r1, p, BLK[4], 13, right_x)
        go(r1, p, BLK[4], 14, left_x)
        share(p, 0, 4)

    def middle(p):
        got(r1, p, BLK[1], 9)
        go(r1, p, BLK[1], 11, right_x, HALF[0])
        share(p, 0, 1)
        got(r1, p, BLK[2], 10)
        go(r1, p, BLK[2], 12, left_x, HALF[1])
        share(p, 0, 2)
        got(r2, p, BLK[3], 2, HALF[0])
        got(r2, p, BLK[3], 3, HALF[1])
        go(r2, p, BLK[3], 7, over_z)
        share(p, 1, 3)
        got(r2, p, BLK[4], 4)
        share(p, 1, 4)

    def late(p):
        got(r1, p, BLK[5], 13)
        go(r1, p, BLK[5], 15, right_x, HALF[0])
        share(p, 0, 5)
        got(r1, p, BLK[6], 14)
        go(r1, p, BLK[6], 16, left_x, HALF[1])
        share(p, 0, 6)
        got(r1, p, BLK[3], 11, HALF[0])
        got(r1, p, BLK[3], 12, HALF[1])
        share(p, 0, 3)
        got(r2, p, BLK[5], 5)
        share(p, 1, 5)
        got(r2, p, BLK[6], 6)
        share(p, 1, 6)

    def last(p):
        got(r2, p, BLK[7], 7)
        share(p, 1, 7)
        got(r1, p, BLK[7], 15, HALF[0])
        got(r1, p, BLK[7], 16, HALF[1])
        share(p, 0, 7)

    def shared(p):
        for route in range(2):
            for i in range(8):
                got((r1, r2)[route], p, BLK[i], 17 + route * 8 + i, half=co)

    pack(0)
    copies.arrived(lefts.at[col_of(y, zlo)], L0 + 2, sibling)
    other = lefts.at[col_of(y, zlo)]
    copies.start(other, other, L0 + 5, right_y)
    copies.start(other, other, L0 + 6, left_y)
    early(0)
    pack(1)
    pick_left(col_of(y, zlo))
    middle(0)
    early(1)
    c_l, c_r, c_o = col_of(yl, zlo), col_of(yr, zlo), col_of(yo, zlo)
    copies.arrived(lefts.at[c_l], L0 + 5, sibling)
    copies.start(lefts.at[c_l, 0], lefts.at[c_l, 0], L0 + 7, right_y)
    copies.arrived(lefts.at[c_r], L0 + 6, sibling)
    copies.start(lefts.at[c_r, 1], lefts.at[c_r, 1], L0 + 8, left_y)
    late(0)
    own_o = col_of(yo, zl)
    copies.arrived(lefts.at[own_o, 0], L0 + 3, sibling)
    copies.arrived(lefts.at[own_o, 1], L0 + 4, sibling)
    pick_left(own_o)
    pick_left(c_l)
    pick_left(c_r)
    middle(1)
    last(0)
    shared(0)
    copies.arrived(lefts.at[c_o, 0], L0 + 7, sibling)
    copies.arrived(lefts.at[c_o, 1], L0 + 8, sibling)
    pick_left(c_o)
    late(1)
    local[6].wait()
    for h, route, lo, hi in slices(r1.shape[4], r2.shape[4]):
        merge_slice(0, h, route, lo, hi, base_first, packed_left, r1, r2, merged)
    last(1)
    shared(1)
    local[7].wait()
    copies.finish()


def slices(width1, width2, step=384):
    cut = []
    for h in range(2):
        for route, width in enumerate((width1, width2)):
            for lo in range(0, width, step):
                cut.append((h, route, lo, min(lo + step, width)))
    return cut


def columns_of(h, route, lo, hi, width1, half):
    start = h * half + route * width1 + lo
    return slice(start, start + hi - lo)


def merge_slice(p, h, route, lo, hi, base, packed_left, r1, r2, out):
    rhs = (r1, r2)[route][h, :, p, :, lo:hi].reshape(packed_left.shape[2], hi - lo)
    delta = jnp.dot(packed_left[p], rhs, preferred_element_type=F32)
    cols = columns_of(h, route, lo, hi, r1.shape[4], base.shape[1] // 2)
    out[:, cols] = (base[:, cols].astype(F32) + delta).astype(BF16)


def merge_kernel(merged, base_last, packed_left, r1, r2, out, last, sems):
    width1, half = r1.shape[4], base_last.shape[1] // 2
    started = [pltpu.make_async_copy(merged, out.at[0], sems.at[0])]
    started[0].start()
    for n, (h, route, lo, hi) in enumerate(slices(width1, r2.shape[4])):
        merge_slice(1, h, route, lo, hi, base_last, packed_left, r1, r2, last)
        cols = columns_of(h, route, lo, hi, width1, half)
        copy = pltpu.make_async_copy(last.at[:, cols], out.at[1, :, cols], sems.at[n + 1])
        copy.start()
        started.append(copy)
    for copy in started:
        copy.wait()


def body(base, left, right, ranks, steps, slots):
    projections, rows, columns = base.shape
    half = columns // 2
    left = left.reshape(projections, rows, 128)
    right = right.reshape(projections, 8, UNIT, half)
    w1 = ROUTE1_TILES * 128
    w2 = half - w1
    vmem = pl.BlockSpec(memory_space=pltpu.VMEM)
    hbm = pl.BlockSpec(memory_space=pltpu.HBM)
    r1, r2, packed_left, merged, base_last = pl.pallas_call(
        gather_kernel,
        out_shape=(
            jax.ShapeDtypeStruct((2, 8, 2, 64, w1), BF16),
            jax.ShapeDtypeStruct((2, 8, 2, 64, w2), BF16),
            jax.ShapeDtypeStruct((2, rows, 512), BF16),
            jax.ShapeDtypeStruct((rows, columns), BF16),
            jax.ShapeDtypeStruct((rows, columns), BF16),
        ),
        in_specs=[hbm] * 6,
        out_specs=(vmem,) * 5,
        scratch_shapes=[
            pltpu.SMEM((SLOTS,), jnp.int32),
            pltpu.SMEM((SLOTS,), jnp.int32),
            pltpu.SMEM((SLOTS,), jnp.int32),
            pltpu.VMEM((8, UNIT, half), BF16),
            pltpu.VMEM((8, UNIT, half), BF16),
            pltpu.VMEM((rows, columns), BF16),
            pltpu.VMEM((2, 8, UNIT, half), BF16),
            pltpu.VMEM((2, 4, 2, UNIT, half), BF16),
            pltpu.VMEM((4, 2, UNIT, half), BF16),
            pltpu.VMEM((4, 2, UNIT, half), BF16),
            pltpu.VMEM((8, 2, rows, 128), BF16),
            pltpu.SemaphoreType.DMA((N_SEND,)),
            pltpu.SemaphoreType.DMA((N_RECV,)),
            pltpu.SemaphoreType.DMA((8,)),
        ],
        compiler_params=pltpu.CompilerParams(
            collective_id=0, has_side_effects=True, vmem_limit_bytes=32 * 2**20
        ),
        name="gather_factors",
    )(*[pltpu.with_memory_space_constraint(a, pltpu.HBM) for a in (ranks, steps, slots, left, right)], base)
    return pl.pallas_call(
        merge_kernel,
        out_shape=jax.ShapeDtypeStruct(base.shape, BF16),
        in_specs=[vmem] * 5,
        out_specs=pl.BlockSpec(memory_space=pltpu.HBM),
        scratch_shapes=[
            pltpu.VMEM((rows, columns), BF16),
            pltpu.SemaphoreType.DMA((1 + len(slices(w1, w2)),)),
        ],
        compiler_params=pltpu.CompilerParams(vmem_limit_bytes=24 * 2**20),
        name="merge_blocks",
    )(merged, base_last, packed_left, r1, r2)


def solution(mesh):
    placed = (P(None, "row", "col"), P(None, "row", "col", None), P(None, "col", None, "row"), P(), P(), P())
    return jax.shard_map(
        body, mesh=mesh, in_specs=placed, out_specs=P(None, "row", "col"), check_vma=False
    )
```

```python
import functools

import jax
import jax.numpy as jnp
from jax import lax
from jax.experimental import pallas as pl
from jax.experimental.pallas import tpu as pltpu
from jax.sharding import PartitionSpec as P

ADAPTER_ALPHA = 32
MESH = pl.DeviceIdType.MESH
BF16 = jnp.bfloat16
F32 = jnp.float32
SLOTS = 8
UNIT = 16
DRAIN = 0
CHUNKS = 2
ROUTE1_TILES = 9
FIRST = (0, 1)
PACED = {}
SCHEDULE = (
    "T0", "L1", "T1", "P0", "L0", "P1", "K0", "E0", "L3", "M0", "L2", "E1", "A0", "K1", "K2",
    "K4", "M1", "L4", "L5", "K3", "Z0", "A1", "K5", "K6", "L6", "K7", "L7", "H0", "G0", "Z1",
    "H1",
)


def slot_ends(ranks, slots):
    ends, total = [], jnp.int32(0)
    for s in range(SLOTS):
        for w in range(SLOTS):
            total = total + jnp.where(slots[w] == s, ranks[w], 0)
        ends.append(total // UNIT)
    return ends


def slot_and_start(position, ends):
    slot = jnp.zeros_like(position)
    start = jnp.zeros_like(position)
    for s in range(SLOTS - 1):
        past = position >= ends[s]
        slot = slot + jnp.where(past, 1, 0)
        start = jnp.where(past, ends[s], start)
    return slot, start


class Copies:
    def __init__(self, send_sems, recv_sems):
        self.send_sems, self.recv_sems = send_sems, recv_sems
        self.count, self.started = 0, []

    def start(self, src, dst, event, device):
        copy = pltpu.make_async_remote_copy(
            src_ref=src,
            dst_ref=dst,
            send_sem=self.send_sems.at[self.count],
            recv_sem=self.recv_sems.at[event],
            device_id=device,
            device_id_type=MESH,
        )
        self.count += 1
        copy.start()
        self.started.append((copy, None))

    def start_or_local(self, src, dst, event, device, local):
        copy = pltpu.make_async_remote_copy(
            src_ref=src,
            dst_ref=dst,
            send_sem=self.send_sems.at[self.count],
            recv_sem=self.recv_sems.at[event],
            device_id=device,
            device_id_type=MESH,
        )
        own = pltpu.make_async_copy(src, dst, self.recv_sems.at[event])
        self.count += 1
        remote = jnp.logical_not(local)
        pl.when(remote)(copy.start)
        pl.when(local)(own.start)
        self.started.append((copy, remote))

    def arrived(self, dst, event, device):
        pltpu.make_async_remote_copy(
            src_ref=dst,
            dst_ref=dst,
            send_sem=self.send_sems.at[0],
            recv_sem=self.recv_sems.at[event],
            device_id=device,
            device_id_type=MESH,
        ).wait_recv()

    def drain(self, count):
        for copy, when in self.started[:count]:
            if when is None:
                copy.wait_send()
            else:
                pl.when(when)(copy.wait_send)
        self.started = self.started[count:]

    def finish(self):
        for copy, when in self.started:
            if when is None:
                copy.wait_send()
            else:
                pl.when(when)(copy.wait_send)


N_A1, N_A2, N_L, N_B = CHUNKS * 8, CHUNKS * 4, 9, 17 + 16
N_RECV = N_A1 + N_A2 + N_L + CHUNKS * N_B
N_SEND = CHUNKS * (8 + 3 + N_B) + 9


def gather_kernel(
    ranks_hbm,
    steps_hbm,
    slots_hbm,
    left,
    right_hbm,
    base,
    r1,
    r2,
    packed_left,
    work,
    ranks,
    steps,
    slots,
    right0,
    right1,
    staged,
    first,
    *rest,
):
    second, (lefts, send_sems, recv_sems, own_sems) = rest[:CHUNKS], rest[CHUNKS:]
    row, col = lax.axis_index("row"), lax.axis_index("col")
    x, zh, core = row // 4, (row // 2) % 2, row % 2
    zl, y = col // 4, col % 4
    t = row // 2

    def dev(x_=x, zh_=zh, core_=core, y_=y, zl_=zl):
        return (x_ * 4 + zh_ * 2 + core_, zl_ * 4 + y_)

    xr, xl, xo = (x + 1) % 4, (x + 3) % 4, (x + 2) % 4
    yr, yl, yo = (y + 1) % 4, (y + 3) % 4, (y + 2) % 4
    zo, co, zlo = 1 - zh, 1 - core, 1 - zl
    right_x, left_x = dev(x_=xr), dev(x_=xl)
    right_y, left_y = dev(y_=yr), dev(y_=yl)
    over_z, sibling, over_zl = dev(zh_=zo), dev(core_=co), dev(zl_=zlo)

    barrier = pltpu.get_barrier_semaphore()
    greeted = [right_x, left_x, over_z, sibling, over_zl, right_y, left_y, dev(y_=yo)]
    for a in range(2):
        for zh0 in range(2):
            for zl0 in range(2):
                greeted.append(dev(x_=2 * zl + a, zh_=zh0, zl_=zl0))
    for device in greeted:
        pl.semaphore_signal(barrier, inc=1, device_id=device, device_id_type=MESH)

    copies = Copies(send_sems, recv_sems)
    right = (right0, right1)
    chunk_width = staged.shape[3]
    pairs = (
        (ranks_hbm, ranks),
        (steps_hbm, steps),
        (slots_hbm, slots),
        (right_hbm.at[0], right[0]),
        (right_hbm.at[1], right[1]),
        (left, lefts.at[col]),
        (base.at[0], work.at[0]),
        (base.at[1], work.at[1]),
    )
    local = [pltpu.make_async_copy(src, dst, own_sems.at[n]) for n, (src, dst) in enumerate(pairs)]
    for copy in local[:6]:
        copy.start()
    for copy in local[:3]:
        copy.wait()

    ends = slot_ends(ranks, slots)
    own_rank, own_steps, all_steps = jnp.int32(0), jnp.int32(0), jnp.int32(0)
    for w in range(SLOTS):
        mine = slots[w] == col
        own_rank = own_rank + jnp.where(mine, ranks[w], 0)
        own_steps = own_steps + jnp.where(mine, steps[w], 0)
        all_steps = all_steps + steps[w]
    own_start = jnp.int32(0)
    for s in range(SLOTS - 1):
        own_start = jnp.where(col == s + 1, ends[s], own_start)

    def as_vector(v):
        return jnp.full((1, 128), v, jnp.int32).astype(F32)

    scale = ADAPTER_ALPHA * (as_vector(own_steps) / as_vector(all_steps)) / as_vector(own_rank)
    scale = jnp.concatenate([scale] * (chunk_width // 128), axis=1)

    ystar, zlstar = 2 * (x % 2) + zh, x // 2

    def a1_event(p, ystar_, zl_):
        return (p * 4 + ystar_) * 2 + zl_

    def stage(c):
        p, lo = place(c, chunk_width)
        if lo == 0:
            local[3 + p].wait()
        for t2 in range(8):
            k = jnp.bitwise_and(t2 - own_start + 64, 7)
            staged[c, t2] = (right[p][k][:, lo : lo + chunk_width].astype(F32) * scale).astype(BF16)

    def send_unit(c, n):
        dx, dz = (2, 1, 3, 0)[n % 4], n // 4
        x2, zh2 = (x + dx) % 4, (zh + dz) % 2
        src, dst = staged.at[c, x2 * 2 + zh2], first.at[c, ystar, zl]
        event, device = a1_event(c, ystar, zl), dev(x_=x2, zh_=zh2, zl_=zlstar)
        if dx == 0 and dz == 0:
            copies.start_or_local(src, dst, event, device, zl == zlstar)
        else:
            copies.start(src, dst, event, device)

    stage(0)
    pl.semaphore_wait(barrier, len(greeted))

    def send_units(c):
        if c:
            stage(c)
            copies.drain(DRAIN)
        for n in range(8):
            send_unit(c, n)

    for c in FIRST:
        send_units(c)
    for c in range(CHUNKS):
        if c not in FIRST:
            stage(c)
    L0 = N_A1 + N_A2
    own_left = lefts.at[col]
    local[5].wait()
    local[6].start()
    local[7].start()

    depth = packed_left.shape[2]
    lane = lax.broadcasted_iota(jnp.int32, (1, depth), 1)
    position = lane // 64 + 8 * ((lane // UNIT) % 4)
    lane_slot, lane_start = slot_and_start(position, ends)
    source = lane_slot * 128 + (position - lane_start) * UNIT + lane % UNIT

    def pick_left(slot, init=False):
        k = lax.broadcasted_iota(jnp.int32, (128, depth), 0) + slot * 128
        pick = jnp.where(k == source, 1.0, 0.0).astype(BF16)
        for p in range(2):
            part = jnp.dot(lefts[slot, p], pick, preferred_element_type=F32).astype(BF16)
            packed_left[p] = part if init else packed_left[p] + part

    pick_left(col, init=True)

    def a2_event(p, y_):
        return N_A1 + p * 4 + y_

    def turn(c):
        for n, dy in enumerate((2, 1, 3, 0)):
            y2 = (y + dy) % 4
            for zl0 in range(2):
                copies.arrived(first.at[c, y2, zl0], a1_event(c, y2, zl0), sibling)
            if dy:
                copies.start(first.at[c, y2], second[c].at[y], a2_event(c, y), dev(y_=y2))
            else:
                second[c][y] = first[c, y]
            if c in PACED:
                send_unit(PACED[c], 2 * n)
                send_unit(PACED[c], 2 * n + 1)

    def col_of(y_, zl_):
        return zl_ * 4 + y_

    def pass_left(base, zl_):
        c_from_left, c_from_right = col_of(yl, zl_), col_of(yr, zl_)
        copies.arrived(lefts.at[c_from_left], L0 + base, sibling)
        copies.start(lefts.at[c_from_left, 0], lefts.at[c_from_left, 0], L0 + base + 3, right_y)
        copies.arrived(lefts.at[c_from_right], L0 + base + 1, sibling)
        copies.start(lefts.at[c_from_right, 1], lefts.at[c_from_right, 1], L0 + base + 4, left_y)


    BLK = [t, xl * 2 + zh, xr * 2 + zh, xo * 2 + zh, x * 2 + zo, xl * 2 + zo, xr * 2 + zo, xo * 2 + zo]
    HALF = [pl.ds(0, 32), pl.ds(32, 32)]

    def b_event(p, n):
        return N_A1 + N_A2 + N_L + p * N_B + n

    def at(ref, p, blk, rows=None, half=core):
        return ref.at[p, half, blk] if rows is None else ref.at[p, half, blk, rows]

    def go(ref, p, blk, n, device, rows=None):
        copies.start(at(ref, p, blk, rows), at(ref, p, blk, rows), b_event(p, n), device)

    def got(ref, p, blk, n, rows=None, half=core):
        copies.arrived(at(ref, p, blk, rows, half), b_event(p, n), sibling)

    def share(p, route, i):
        go((r1, r2)[route], p, BLK[i], 17 + route * 8 + i, sibling)

    def pack(p):
        for y0 in (1, 2, 3):
            y2 = (y + y0) % 4
            copies.arrived(second[p].at[y2], a2_event(p, y2), sibling)
        width = r1.shape[4]
        for i in range(4):
            slot, _ = slot_and_start(t + 8 * i, ends)
            unit = second[p][jnp.bitwise_and(slot, 3), jnp.right_shift(slot, 2)]
            r1[p, core, t, pl.ds(UNIT * i, UNIT)] = unit[:, :width]
            r2[p, core, t, pl.ds(UNIT * i, UNIT)] = unit[:, width:]
        go(r2, p, t, 0, right_x)
        go(r2, p, t, 1, left_x)
        go(r1, p, t, 8, over_z)
        go(r1, p, t, 9, right_x)
        go(r1, p, t, 10, left_x)
        go(r2, p, t, 4, over_z)
        share(p, 0, 0)
        share(p, 1, 0)

    def early(p):
        got(r2, p, BLK[1], 0)
        go(r2, p, BLK[1], 2, right_x, HALF[0])
        go(r2, p, BLK[1], 5, over_z)
        share(p, 1, 1)
        got(r2, p, BLK[2], 1)
        go(r2, p, BLK[2], 3, left_x, HALF[1])
        go(r2, p, BLK[2], 6, over_z)
        share(p, 1, 2)
        got(r1, p, BLK[4], 8)
        go(r1, p, BLK[4], 13, right_x)
        go(r1, p, BLK[4], 14, left_x)
        share(p, 0, 4)

    def middle(p):
        got(r1, p, BLK[1], 9)
        go(r1, p, BLK[1], 11, right_x, HALF[0])
        share(p, 0, 1)
        got(r1, p, BLK[2], 10)
        go(r1, p, BLK[2], 12, left_x, HALF[1])
        share(p, 0, 2)
        got(r2, p, BLK[3], 2, HALF[0])
        got(r2, p, BLK[3], 3, HALF[1])
        go(r2, p, BLK[3], 7, over_z)
        share(p, 1, 3)
        got(r2, p, BLK[4], 4)
        share(p, 1, 4)

    def late(p):
        got(r1, p, BLK[5], 13)
        go(r1, p, BLK[5], 15, right_x, HALF[0])
        share(p, 0, 5)
        got(r1, p, BLK[6], 14)
        go(r1, p, BLK[6], 16, left_x, HALF[1])
        share(p, 0, 6)
        got(r1, p, BLK[3], 11, HALF[0])
        got(r1, p, BLK[3], 12, HALF[1])
        share(p, 0, 3)
        got(r2, p, BLK[5], 5)
        share(p, 1, 5)
        got(r2, p, BLK[6], 6)
        share(p, 1, 6)

    def last(p):
        got(r2, p, BLK[7], 7)
        share(p, 1, 7)
        got(r1, p, BLK[7], 15, HALF[0])
        got(r1, p, BLK[7], 16, HALF[1])
        share(p, 0, 7)

    def shared(p):
        for route in range(2):
            for i in range(8):
                got((r1, r2)[route], p, BLK[i], 17 + route * 8 + i, half=co)

    def start_left():
        copies.start(own_left, own_left, L0 + 0, right_y)
        copies.start(own_left, own_left, L0 + 1, left_y)

    def cross_left():
        other = lefts.at[col_of(y, zlo)]
        copies.arrived(other, L0 + 2, sibling)
        copies.start(other, other, L0 + 5, right_y)
        copies.start(other, other, L0 + 6, left_y)

    c_l, c_r, c_o, own_o = col_of(yl, zlo), col_of(yr, zlo), col_of(yo, zlo), col_of(yo, zl)

    def pass_other_left():
        copies.arrived(lefts.at[c_l], L0 + 5, sibling)
        copies.start(lefts.at[c_l, 0], lefts.at[c_l, 0], L0 + 7, right_y)
        copies.arrived(lefts.at[c_r], L0 + 6, sibling)
        copies.start(lefts.at[c_r, 1], lefts.at[c_r, 1], L0 + 8, left_y)

    def merge(c):
        for h, route, lo, hi in slices(r1.shape[4], r2.shape[4]):
            merge_slice(c, h, route, lo, hi, work, packed_left, r1, r2)

    def own_halves():
        copies.arrived(lefts.at[own_o, 0], L0 + 3, sibling)
        copies.arrived(lefts.at[own_o, 1], L0 + 4, sibling)

    def other_halves():
        copies.arrived(lefts.at[c_o, 0], L0 + 7, sibling)
        copies.arrived(lefts.at[c_o, 1], L0 + 8, sibling)

    def load_base():
        local[6].wait()
        local[7].wait()

    steps_of = {
        "T": turn, "P": pack, "E": early, "M": middle, "A": late, "Z": last, "H": shared, "G": merge,
        "L": lambda n: (
            start_left,
            lambda: copies.start(own_left, own_left, L0 + 2, over_zl),
            lambda: pass_left(0, zl),
            cross_left,
            pass_other_left,
            own_halves,
            other_halves,
            load_base,
        )[n](),
        "K": lambda n: pick_left(
            (col, col_of(yl, zl), col_of(yr, zl), own_o, col_of(y, zlo), c_l, c_r, c_o)[n], init=n == 0
        ),
    }
    for step in SCHEDULE:
        steps_of[step[0]](int(step[1]))
    copies.finish()


def place(chunk, width):
    per = CHUNKS // 2
    return chunk // per, (chunk % per) * width


def slices(width1, width2, step=512):
    cut = []
    for h in range(2):
        for route, width in enumerate((width1, width2)):
            for lo in range(0, width, step):
                cut.append((h, route, lo, min(lo + step, width)))
    return cut


def merge_slice(c, h, route, lo, hi, work, packed_left, r1, r2, out=None):
    width1, half = r1.shape[4], work.shape[2] // 2
    p, first = place(c, width1 + r2.shape[4])
    begin = h * half + first + route * width1 + lo
    cols = slice(begin, begin + hi - lo)
    rhs = (r1, r2)[route][c, h, :, :, lo:hi].reshape(packed_left.shape[2], hi - lo)
    delta = jnp.dot(packed_left[p], rhs, preferred_element_type=F32)
    total = (work[p, :, cols].astype(F32) + delta).astype(BF16)
    if out is None:
        work[p, :, cols] = total
    else:
        out[:, cols] = total
    return p, cols


def merge_kernel(work, packed_left, r1, r2, out, last, sems):
    width1, width2, half = r1.shape[4], r2.shape[4], work.shape[2] // 2
    p, lo = place(CHUNKS - 1, width1 + width2)
    pairs = [(work.at[p2], out.at[p2]) for p2 in range(p)]
    for h in range(2 if lo else 0):
        cols = slice(h * half, h * half + lo)
        pairs.append((work.at[p, :, cols], out.at[p, :, cols]))
    started = []

    def send(src, dst):
        copy = pltpu.make_async_copy(src, dst, sems.at[len(started)])
        copy.start()
        started.append(copy)

    for src, dst in pairs:
        send(src, dst)
    for h, route, lo, hi in slices(width1, width2):
        p, cols = merge_slice(CHUNKS - 1, h, route, lo, hi, work, packed_left, r1, r2, last)
        send(last.at[:, cols], out.at[p, :, cols])
    for copy in started:
        copy.wait()


def body(base, left, right, ranks, steps, slots):
    projections, rows, columns = base.shape
    half = columns // 2
    left = left.reshape(projections, rows, 128)
    right = right.reshape(projections, 8, UNIT, half)
    width = 2 * half // CHUNKS
    w1 = ROUTE1_TILES * 128
    w2 = width - w1
    vmem = pl.BlockSpec(memory_space=pltpu.VMEM)
    hbm = pl.BlockSpec(memory_space=pltpu.HBM)
    r1, r2, packed_left, work = pl.pallas_call(
        gather_kernel,
        out_shape=(
            jax.ShapeDtypeStruct((CHUNKS, 2, 8, 64, w1), BF16),
            jax.ShapeDtypeStruct((CHUNKS, 2, 8, 64, w2), BF16),
            jax.ShapeDtypeStruct((2, rows, 512), BF16),
            jax.ShapeDtypeStruct(base.shape, BF16),
        ),
        in_specs=[hbm] * 6,
        out_specs=(vmem,) * 4,
        scratch_shapes=[
            pltpu.SMEM((SLOTS,), jnp.int32),
            pltpu.SMEM((SLOTS,), jnp.int32),
            pltpu.SMEM((SLOTS,), jnp.int32),
            pltpu.VMEM((8, UNIT, half), BF16),
            pltpu.VMEM((8, UNIT, half), BF16),
            pltpu.VMEM((CHUNKS, 8, UNIT, width), BF16),
            pltpu.VMEM((CHUNKS, 4, 2, UNIT, width), BF16),
            *[pltpu.VMEM((4, 2, UNIT, width), BF16)] * CHUNKS,
            pltpu.VMEM((8, 2, rows, 128), BF16),
            pltpu.SemaphoreType.DMA((N_SEND,)),
            pltpu.SemaphoreType.DMA((N_RECV,)),
            pltpu.SemaphoreType.DMA((8,)),
        ],
        compiler_params=pltpu.CompilerParams(
            collective_id=0, has_side_effects=True, vmem_limit_bytes=24 * 2**20
        ),
        name="gather_factors",
    )(*[pltpu.with_memory_space_constraint(a, pltpu.HBM) for a in (ranks, steps, slots, left, right, base)])
    return pl.pallas_call(
        merge_kernel,
        out_shape=jax.ShapeDtypeStruct(base.shape, BF16),
        in_specs=[vmem] * 4,
        out_specs=pl.BlockSpec(memory_space=pltpu.HBM),
        scratch_shapes=[pltpu.VMEM((rows, columns), BF16), pltpu.SemaphoreType.DMA((16,))],
        compiler_params=pltpu.CompilerParams(vmem_limit_bytes=24 * 2**20),
        name="merge_blocks",
    )(work, packed_left, r1, r2)


def solution(mesh):
    placed = (P(None, "row", "col"), P(None, "row", "col", None), P(None, "col", None, "row"), P(), P(), P())
    return jax.shard_map(
        body, mesh=mesh, in_specs=placed, out_specs=P(None, "row", "col"), check_vma=False
    )
```

```python
import functools

import jax
import jax.numpy as jnp
from jax import lax
from jax.experimental import pallas as pl
from jax.experimental.pallas import tpu as pltpu
from jax.sharding import PartitionSpec as P

ADAPTER_ALPHA = 32
MESH = pl.DeviceIdType.MESH
BF16 = jnp.bfloat16
F32 = jnp.float32
SLOTS = 8
UNIT = 16
DRAIN = 7
CHUNKS = 2
ROUTE1_TILES = 8
FIRST = (0, 1)
PACED = {}
SCHEDULE = (
    "T0", "L1", "T1", "P0", "P1", "L0", "K0", "E0", "L3", "M0", "E1", "L2", "A0", "L4", "K1",
    "K2", "K4", "D2", "M1", "L5", "K3", "Z0", "A1", "K5", "K6", "L6", "K7", "L7", "H0", "I0",
    "J0", "D4", "H1", "G0", "D2", "I1", "D1", "Z1", "J1",
)


def slot_ends(ranks, slots):
    ends, total = [], jnp.int32(0)
    for s in range(SLOTS):
        for w in range(SLOTS):
            total = total + jnp.where(slots[w] == s, ranks[w], 0)
        ends.append(total // UNIT)
    return ends


def slot_and_start(position, ends):
    slot = jnp.zeros_like(position)
    start = jnp.zeros_like(position)
    for s in range(SLOTS - 1):
        past = position >= ends[s]
        slot = slot + jnp.where(past, 1, 0)
        start = jnp.where(past, ends[s], start)
    return slot, start


class Copies:
    def __init__(self, send_sems, recv_sems):
        self.send_sems, self.recv_sems = send_sems, recv_sems
        self.count, self.started = 0, []

    def start(self, src, dst, event, device):
        copy = pltpu.make_async_remote_copy(
            src_ref=src,
            dst_ref=dst,
            send_sem=self.send_sems.at[self.count],
            recv_sem=self.recv_sems.at[event],
            device_id=device,
            device_id_type=MESH,
        )
        self.count += 1
        copy.start()
        self.started.append((copy, None))

    def start_or_local(self, src, dst, event, device, local):
        copy = pltpu.make_async_remote_copy(
            src_ref=src,
            dst_ref=dst,
            send_sem=self.send_sems.at[self.count],
            recv_sem=self.recv_sems.at[event],
            device_id=device,
            device_id_type=MESH,
        )
        own = pltpu.make_async_copy(src, dst, self.recv_sems.at[event])
        self.count += 1
        remote = jnp.logical_not(local)
        pl.when(remote)(copy.start)
        pl.when(local)(own.start)
        self.started.append((copy, remote))

    def arrived(self, dst, event, device):
        pltpu.make_async_remote_copy(
            src_ref=dst,
            dst_ref=dst,
            send_sem=self.send_sems.at[0],
            recv_sem=self.recv_sems.at[event],
            device_id=device,
            device_id_type=MESH,
        ).wait_recv()

    def drain(self, count):
        for copy, when in self.started[:count]:
            if when is None:
                copy.wait_send()
            else:
                pl.when(when)(copy.wait_send)
        self.started = self.started[count:]

    def finish(self):
        for copy, when in self.started:
            if when is None:
                copy.wait_send()
            else:
                pl.when(when)(copy.wait_send)


N_A1, N_A2, N_L, N_B = CHUNKS * 8, CHUNKS * 4, 9, 17 + 16
N_RECV = N_A1 + N_A2 + N_L + CHUNKS * N_B
N_SEND = CHUNKS * (8 + 3 + N_B) + 9


def gather_kernel(
    ranks_hbm,
    steps_hbm,
    slots_hbm,
    left,
    right_hbm,
    base,
    r1,
    r2,
    packed_left,
    work,
    ranks,
    steps,
    slots,
    right0,
    right1,
    staged,
    first,
    *rest,
):
    second, (lefts, send_sems, recv_sems, own_sems) = rest[:CHUNKS], rest[CHUNKS:]
    row, col = lax.axis_index("row"), lax.axis_index("col")
    x, zh, core = row // 4, (row // 2) % 2, row % 2
    zl, y = col // 4, col % 4
    t = row // 2

    def dev(x_=x, zh_=zh, core_=core, y_=y, zl_=zl):
        return (x_ * 4 + zh_ * 2 + core_, zl_ * 4 + y_)

    xr, xl, xo = (x + 1) % 4, (x + 3) % 4, (x + 2) % 4
    yr, yl, yo = (y + 1) % 4, (y + 3) % 4, (y + 2) % 4
    zo, co, zlo = 1 - zh, 1 - core, 1 - zl
    right_x, left_x = dev(x_=xr), dev(x_=xl)
    right_y, left_y = dev(y_=yr), dev(y_=yl)
    over_z, sibling, over_zl = dev(zh_=zo), dev(core_=co), dev(zl_=zlo)

    barrier = pltpu.get_barrier_semaphore()
    greeted = []
    for a in range(2):
        for zh0 in range(2):
            for zl0 in range(2):
                greeted.append(dev(x_=2 * zl + a, zh_=zh0, zl_=zl0))
    greeted += [right_x, left_x, over_z, sibling, over_zl, right_y, left_y, dev(y_=yo)]
    for device in greeted:
        pl.semaphore_signal(barrier, inc=1, device_id=device, device_id_type=MESH)

    copies = Copies(send_sems, recv_sems)
    right = (right0, right1)
    chunk_width = staged.shape[3]
    pairs = (
        (ranks_hbm, ranks),
        (steps_hbm, steps),
        (slots_hbm, slots),
        (right_hbm.at[0], right[0]),
        (right_hbm.at[1], right[1]),
        (left, lefts.at[col]),
        (base.at[0], work.at[0]),
        (base.at[1], work.at[1]),
    )
    local = [pltpu.make_async_copy(src, dst, own_sems.at[n]) for n, (src, dst) in enumerate(pairs)]
    for copy in local[:6]:
        copy.start()
    for copy in local[:3]:
        copy.wait()

    ends = slot_ends(ranks, slots)
    own_rank, own_steps, all_steps = jnp.int32(0), jnp.int32(0), jnp.int32(0)
    for w in range(SLOTS):
        mine = slots[w] == col
        own_rank = own_rank + jnp.where(mine, ranks[w], 0)
        own_steps = own_steps + jnp.where(mine, steps[w], 0)
        all_steps = all_steps + steps[w]
    own_start = jnp.int32(0)
    for s in range(SLOTS - 1):
        own_start = jnp.where(col == s + 1, ends[s], own_start)

    def as_vector(v):
        return jnp.full((1, 128), v, jnp.int32).astype(F32)

    scale = ADAPTER_ALPHA * (as_vector(own_steps) / as_vector(all_steps)) / as_vector(own_rank)
    scale = jnp.concatenate([scale] * (chunk_width // 128), axis=1)

    ystar, zlstar = 2 * (x % 2) + zh, x // 2

    def a1_event(p, ystar_, zl_):
        return (p * 4 + ystar_) * 2 + zl_

    def stage(c):
        p, lo = place(c, chunk_width)
        if lo == 0:
            local[3 + p].wait()
        for t2 in range(8):
            k = jnp.bitwise_and(t2 - own_start + 64, 7)
            staged[c, t2] = (right[p][k][:, lo : lo + chunk_width].astype(F32) * scale).astype(BF16)

    def send_unit(c, n):
        dx, dz = (2, 1, 3, 0)[n % 4], n // 4
        x2, zh2 = (x + dx) % 4, (zh + dz) % 2
        src, dst = staged.at[c, x2 * 2 + zh2], first.at[c, ystar, zl]
        event, device = a1_event(c, ystar, zl), dev(x_=x2, zh_=zh2, zl_=zlstar)
        if dx == 0 and dz == 0:
            copies.start_or_local(src, dst, event, device, zl == zlstar)
        else:
            copies.start(src, dst, event, device)

    stage(0)
    pl.semaphore_wait(barrier, len(greeted))

    def send_units(c):
        if c:
            stage(c)
            copies.drain(DRAIN)
        for n in range(8):
            send_unit(c, n)

    for c in FIRST:
        send_units(c)
    for c in range(CHUNKS):
        if c not in FIRST and c in PACED.values():
            stage(c)
    L0 = N_A1 + N_A2
    own_left = lefts.at[col]
    local[5].wait()
    local[6].start()
    local[7].start()

    depth = packed_left.shape[2]
    lane = lax.broadcasted_iota(jnp.int32, (1, depth), 1)
    position = lane // 64 + 8 * ((lane // UNIT) % 4)
    lane_slot, lane_start = slot_and_start(position, ends)
    source = lane_slot * 128 + (position - lane_start) * UNIT + lane % UNIT

    def pick_left(slot, init=False):
        k = lax.broadcasted_iota(jnp.int32, (128, depth), 0) + slot * 128
        pick = jnp.where(k == source, 1.0, 0.0).astype(BF16)
        for p in range(2):
            part = jnp.dot(lefts[slot, p], pick, preferred_element_type=F32).astype(BF16)
            packed_left[p] = part if init else packed_left[p] + part

    pick_left(col, init=True)

    def a2_event(p, y_):
        return N_A1 + p * 4 + y_

    def turn(c):
        for n, dy in enumerate((2, 1, 3, 0)):
            y2 = (y + dy) % 4
            for zl0 in range(2):
                copies.arrived(first.at[c, y2, zl0], a1_event(c, y2, zl0), sibling)
            if dy:
                copies.start(first.at[c, y2], second[c].at[y], a2_event(c, y), dev(y_=y2))
            else:
                second[c][y] = first[c, y]
            if c in PACED:
                send_unit(PACED[c], 2 * n)
                send_unit(PACED[c], 2 * n + 1)

    def col_of(y_, zl_):
        return zl_ * 4 + y_

    def pass_left(base, zl_):
        c_from_left, c_from_right = col_of(yl, zl_), col_of(yr, zl_)
        copies.arrived(lefts.at[c_from_left], L0 + base, sibling)
        copies.start(lefts.at[c_from_left, 0], lefts.at[c_from_left, 0], L0 + base + 3, right_y)
        copies.arrived(lefts.at[c_from_right], L0 + base + 1, sibling)
        copies.start(lefts.at[c_from_right, 1], lefts.at[c_from_right, 1], L0 + base + 4, left_y)


    BLK = [t, xl * 2 + zh, xr * 2 + zh, xo * 2 + zh, x * 2 + zo, xl * 2 + zo, xr * 2 + zo, xo * 2 + zo]
    HALF = [pl.ds(0, 32), pl.ds(32, 32)]

    def b_event(p, n):
        return N_A1 + N_A2 + N_L + p * N_B + n

    def at(ref, p, blk, rows=None, half=core):
        return ref.at[p, half, blk] if rows is None else ref.at[p, half, blk, rows]

    def go(ref, p, blk, n, device, rows=None):
        copies.start(at(ref, p, blk, rows), at(ref, p, blk, rows), b_event(p, n), device)

    def got(ref, p, blk, n, rows=None, half=core):
        copies.arrived(at(ref, p, blk, rows, half), b_event(p, n), sibling)

    def share(p, route, i):
        go((r1, r2)[route], p, BLK[i], 17 + route * 8 + i, sibling)

    def pack(p):
        for y0 in (1, 2, 3):
            y2 = (y + y0) % 4
            copies.arrived(second[p].at[y2], a2_event(p, y2), sibling)
        width = r1.shape[4]
        for i in range(4):
            slot, _ = slot_and_start(t + 8 * i, ends)
            unit = second[p][jnp.bitwise_and(slot, 3), jnp.right_shift(slot, 2)]
            r1[p, core, t, pl.ds(UNIT * i, UNIT)] = unit[:, :width]
            r2[p, core, t, pl.ds(UNIT * i, UNIT)] = unit[:, width:]
        go(r2, p, t, 0, right_x)
        go(r2, p, t, 1, left_x)
        go(r1, p, t, 8, over_z)
        go(r1, p, t, 9, right_x)
        go(r1, p, t, 10, left_x)
        go(r2, p, t, 4, over_z)
        share(p, 0, 0)
        share(p, 1, 0)

    def early(p):
        got(r2, p, BLK[1], 0)
        go(r2, p, BLK[1], 2, right_x, HALF[0])
        go(r2, p, BLK[1], 5, over_z)
        share(p, 1, 1)
        got(r2, p, BLK[2], 1)
        go(r2, p, BLK[2], 3, left_x, HALF[1])
        go(r2, p, BLK[2], 6, over_z)
        share(p, 1, 2)
        got(r1, p, BLK[4], 8)
        go(r1, p, BLK[4], 13, right_x)
        go(r1, p, BLK[4], 14, left_x)
        share(p, 0, 4)

    def middle(p):
        got(r1, p, BLK[1], 9)
        go(r1, p, BLK[1], 11, right_x, HALF[0])
        share(p, 0, 1)
        got(r1, p, BLK[2], 10)
        go(r1, p, BLK[2], 12, left_x, HALF[1])
        share(p, 0, 2)
        got(r2, p, BLK[3], 2, HALF[0])
        got(r2, p, BLK[3], 3, HALF[1])
        go(r2, p, BLK[3], 7, over_z)
        share(p, 1, 3)
        got(r2, p, BLK[4], 4)
        share(p, 1, 4)

    def late(p):
        got(r1, p, BLK[5], 13)
        go(r1, p, BLK[5], 15, right_x, HALF[0])
        share(p, 0, 5)
        got(r1, p, BLK[6], 14)
        go(r1, p, BLK[6], 16, left_x, HALF[1])
        share(p, 0, 6)
        got(r1, p, BLK[3], 11, HALF[0])
        got(r1, p, BLK[3], 12, HALF[1])
        share(p, 0, 3)
        got(r2, p, BLK[5], 5)
        share(p, 1, 5)
        got(r2, p, BLK[6], 6)
        share(p, 1, 6)

    def last(p):
        got(r2, p, BLK[7], 7)
        share(p, 1, 7)
        got(r1, p, BLK[7], 15, HALF[0])
        got(r1, p, BLK[7], 16, HALF[1])
        share(p, 0, 7)

    def shared(p, blocks):
        for i in blocks:
            for route in range(2):
                got((r1, r2)[route], p, BLK[i], 17 + route * 8 + i, half=co)

    def start_left():
        copies.start(own_left, own_left, L0 + 0, right_y)
        copies.start(own_left, own_left, L0 + 1, left_y)

    def cross_left():
        other = lefts.at[col_of(y, zlo)]
        copies.arrived(other, L0 + 2, sibling)
        copies.start(other, other, L0 + 5, right_y)
        copies.start(other, other, L0 + 6, left_y)

    c_l, c_r, c_o, own_o = col_of(yl, zlo), col_of(yr, zlo), col_of(yo, zlo), col_of(yo, zl)

    def pass_other_left():
        copies.arrived(lefts.at[c_l], L0 + 5, sibling)
        copies.start(lefts.at[c_l, 0], lefts.at[c_l, 0], L0 + 7, right_y)
        copies.arrived(lefts.at[c_r], L0 + 6, sibling)
        copies.start(lefts.at[c_r, 1], lefts.at[c_r, 1], L0 + 8, left_y)

    def merge(c):
        for h, route, lo, hi in slices(r1.shape[4], r2.shape[4]):
            merge_slice(c, h, route, lo, hi, work, packed_left, r1, r2)

    def own_halves():
        copies.arrived(lefts.at[own_o, 0], L0 + 3, sibling)
        copies.arrived(lefts.at[own_o, 1], L0 + 4, sibling)

    def other_halves():
        copies.arrived(lefts.at[c_o, 0], L0 + 7, sibling)
        copies.arrived(lefts.at[c_o, 1], L0 + 8, sibling)

    def load_base():
        local[6].wait()
        local[7].wait()

    steps_of = {
        "S": send_units, "T": turn, "P": pack, "E": early, "M": middle, "A": late, "Z": last, "H": lambda c: shared(c, (0, 4, 1, 2)), "I": lambda c: shared(c, (3, 5, 6)), "J": lambda c: shared(c, (7,)),
        "D": lambda n: copies.drain(10 * n), "G": merge,
        "L": lambda n: (
            start_left,
            lambda: copies.start(own_left, own_left, L0 + 2, over_zl),
            lambda: pass_left(0, zl),
            cross_left,
            pass_other_left,
            own_halves,
            other_halves,
            load_base,
        )[n](),
        "K": lambda n: pick_left(
            (col, col_of(yl, zl), col_of(yr, zl), own_o, col_of(y, zlo), c_l, c_r, c_o)[n], init=n == 0
        ),
    }
    for step in SCHEDULE:
        steps_of[step[0]](int(step[1]))
    copies.finish()


def place(chunk, width):
    per = CHUNKS // 2
    return chunk // per, (chunk % per) * width


def slices(width1, width2, step=512):
    cut = []
    for h in range(2):
        for route, width in enumerate((width1, width2)):
            for lo in range(0, width, step):
                cut.append((h, route, lo, min(lo + step, width)))
    return cut


def merge_slice(c, h, route, lo, hi, work, packed_left, r1, r2, out=None):
    width1, half = r1.shape[4], work.shape[2] // 2
    p, first = place(c, width1 + r2.shape[4])
    begin = h * half + first + route * width1 + lo
    cols = slice(begin, begin + hi - lo)
    rhs = (r1, r2)[route][c, h, :, :, lo:hi].reshape(packed_left.shape[2], hi - lo)
    delta = jnp.dot(packed_left[p], rhs, preferred_element_type=F32)
    total = (work[p, :, cols].astype(F32) + delta).astype(BF16)
    if out is None:
        work[p, :, cols] = total
    else:
        out[:, cols] = total
    return p, cols


def merge_kernel(work, packed_left, r1, r2, out, last, sems):
    width1, width2, half = r1.shape[4], r2.shape[4], work.shape[2] // 2
    p, lo = place(CHUNKS - 1, width1 + width2)
    pairs = [(work.at[p2], out.at[p2]) for p2 in range(p)]
    for h in range(2 if lo else 0):
        cols = slice(h * half, h * half + lo)
        pairs.append((work.at[p, :, cols], out.at[p, :, cols]))
    started = []

    def send(src, dst):
        copy = pltpu.make_async_copy(src, dst, sems.at[len(started)])
        copy.start()
        started.append(copy)

    for src, dst in pairs:
        send(src, dst)
    for h, route, lo, hi in slices(width1, width2):
        p, cols = merge_slice(CHUNKS - 1, h, route, lo, hi, work, packed_left, r1, r2, last)
        send(last.at[:, cols], out.at[p, :, cols])
    for copy in started:
        copy.wait()


def body(base, left, right, ranks, steps, slots):
    projections, rows, columns = base.shape
    half = columns // 2
    left = left.reshape(projections, rows, 128)
    right = right.reshape(projections, 8, UNIT, half)
    width = 2 * half // CHUNKS
    w1 = ROUTE1_TILES * 128
    w2 = width - w1
    vmem = pl.BlockSpec(memory_space=pltpu.VMEM)
    hbm = pl.BlockSpec(memory_space=pltpu.HBM)
    r1, r2, packed_left, work = pl.pallas_call(
        gather_kernel,
        out_shape=(
            jax.ShapeDtypeStruct((CHUNKS, 2, 8, 64, w1), BF16),
            jax.ShapeDtypeStruct((CHUNKS, 2, 8, 64, w2), BF16),
            jax.ShapeDtypeStruct((2, rows, 512), BF16),
            jax.ShapeDtypeStruct(base.shape, BF16),
        ),
        in_specs=[hbm] * 6,
        out_specs=(vmem,) * 4,
        scratch_shapes=[
            pltpu.SMEM((SLOTS,), jnp.int32),
            pltpu.SMEM((SLOTS,), jnp.int32),
            pltpu.SMEM((SLOTS,), jnp.int32),
            pltpu.VMEM((8, UNIT, half), BF16),
            pltpu.VMEM((8, UNIT, half), BF16),
            pltpu.VMEM((CHUNKS, 8, UNIT, width), BF16),
            pltpu.VMEM((CHUNKS, 4, 2, UNIT, width), BF16),
            *[pltpu.VMEM((4, 2, UNIT, width), BF16)] * CHUNKS,
            pltpu.VMEM((8, 2, rows, 128), BF16),
            pltpu.SemaphoreType.DMA((N_SEND,)),
            pltpu.SemaphoreType.DMA((N_RECV,)),
            pltpu.SemaphoreType.DMA((8,)),
        ],
        compiler_params=pltpu.CompilerParams(
            collective_id=0, has_side_effects=True, vmem_limit_bytes=24 * 2**20
        ),
        name="gather_factors",
    )(*[pltpu.with_memory_space_constraint(a, pltpu.HBM) for a in (ranks, steps, slots, left, right, base)])
    return pl.pallas_call(
        merge_kernel,
        out_shape=jax.ShapeDtypeStruct(base.shape, BF16),
        in_specs=[vmem] * 4,
        out_specs=pl.BlockSpec(memory_space=pltpu.HBM),
        scratch_shapes=[pltpu.VMEM((rows, columns), BF16), pltpu.SemaphoreType.DMA((16,))],
        compiler_params=pltpu.CompilerParams(vmem_limit_bytes=24 * 2**20),
        name="merge_blocks",
    )(work, packed_left, r1, r2)


def solution(mesh):
    placed = (P(None, "row", "col"), P(None, "row", "col", None), P(None, "col", None, "row"), P(), P(), P())
    return jax.shard_map(
        body, mesh=mesh, in_specs=placed, out_specs=P(None, "row", "col"), check_vma=False
    )
```

```python
import functools

import jax
import jax.numpy as jnp
from jax import lax
from jax.experimental import pallas as pl
from jax.experimental.pallas import tpu as pltpu
from jax.sharding import PartitionSpec as P

ADAPTER_ALPHA = 32
MESH = pl.DeviceIdType.MESH
BF16 = jnp.bfloat16
F32 = jnp.float32
SLOTS = 8
UNIT = 16
DRAIN = 7
CHUNKS = 2
ROUTE1_TILES = 8
FIRST = (0, 1)
PACED = {}
SCHEDULE = (
    "T0", "L1", "T1", "P0", "P1", "L0", "K0", "E0", "L3", "M0", "E1", "L2", "A0", "L4", "K1",
    "K2", "K4", "D2", "M1", "L5", "K3", "Z0", "A1", "K5", "K6", "L6", "K7", "L7", "H0", "I0",
    "J0", "D4", "H1", "G0", "D2", "I1", "D1", "Z1", "J1",
)


def slot_ends(ranks, slots):
    ends, total = [], jnp.int32(0)
    for s in range(SLOTS):
        for w in range(SLOTS):
            total = total + jnp.where(slots[w] == s, ranks[w], 0)
        ends.append(total // UNIT)
    return ends


def slot_and_start(position, ends):
    slot = jnp.zeros_like(position)
    start = jnp.zeros_like(position)
    for s in range(SLOTS - 1):
        past = position >= ends[s]
        slot = slot + jnp.where(past, 1, 0)
        start = jnp.where(past, ends[s], start)
    return slot, start


class Copies:
    def __init__(self, send_sems, recv_sems):
        self.send_sems, self.recv_sems = send_sems, recv_sems
        self.count, self.started = 0, []

    def start(self, src, dst, event, device):
        copy = pltpu.make_async_remote_copy(
            src_ref=src,
            dst_ref=dst,
            send_sem=self.send_sems.at[self.count],
            recv_sem=self.recv_sems.at[event],
            device_id=device,
            device_id_type=MESH,
        )
        self.count += 1
        copy.start()
        self.started.append((copy, None))

    def start_or_local(self, src, dst, event, device, local):
        copy = pltpu.make_async_remote_copy(
            src_ref=src,
            dst_ref=dst,
            send_sem=self.send_sems.at[self.count],
            recv_sem=self.recv_sems.at[event],
            device_id=device,
            device_id_type=MESH,
        )
        own = pltpu.make_async_copy(src, dst, self.recv_sems.at[event])
        self.count += 1
        remote = jnp.logical_not(local)
        pl.when(remote)(copy.start)
        pl.when(local)(own.start)
        self.started.append((copy, remote))

    def arrived(self, dst, event, device):
        pltpu.make_async_remote_copy(
            src_ref=dst,
            dst_ref=dst,
            send_sem=self.send_sems.at[0],
            recv_sem=self.recv_sems.at[event],
            device_id=device,
            device_id_type=MESH,
        ).wait_recv()

    def drain(self, count):
        for copy, when in self.started[:count]:
            if when is None:
                copy.wait_send()
            else:
                pl.when(when)(copy.wait_send)
        self.started = self.started[count:]

    def finish(self):
        for copy, when in self.started:
            if when is None:
                copy.wait_send()
            else:
                pl.when(when)(copy.wait_send)


N_A1, N_A2, N_L, N_B = CHUNKS * 8, CHUNKS * 4, 9, 17 + 8
N_RECV = N_A1 + N_A2 + N_L + CHUNKS * N_B
N_SEND = CHUNKS * (8 + 3 + N_B) + 9


def gather_kernel(
    ranks_hbm,
    steps_hbm,
    slots_hbm,
    left,
    right_hbm,
    base,
    r,
    packed_left,
    work,
    ranks,
    steps,
    slots,
    right0,
    right1,
    staged,
    first,
    *rest,
):
    second, (lefts, send_sems, recv_sems, own_sems) = rest[:CHUNKS], rest[CHUNKS:]
    row, col = lax.axis_index("row"), lax.axis_index("col")
    x, zh, core = row // 4, (row // 2) % 2, row % 2
    zl, y = col // 4, col % 4
    t = row // 2

    def dev(x_=x, zh_=zh, core_=core, y_=y, zl_=zl):
        return (x_ * 4 + zh_ * 2 + core_, zl_ * 4 + y_)

    xr, xl, xo = (x + 1) % 4, (x + 3) % 4, (x + 2) % 4
    yr, yl, yo = (y + 1) % 4, (y + 3) % 4, (y + 2) % 4
    zo, co, zlo = 1 - zh, 1 - core, 1 - zl
    right_x, left_x = dev(x_=xr), dev(x_=xl)
    right_y, left_y = dev(y_=yr), dev(y_=yl)
    over_z, sibling, over_zl = dev(zh_=zo), dev(core_=co), dev(zl_=zlo)

    barrier = pltpu.get_barrier_semaphore()
    greeted = []
    for a in range(2):
        for zh0 in range(2):
            for zl0 in range(2):
                greeted.append(dev(x_=2 * zl + a, zh_=zh0, zl_=zl0))
    greeted += [right_x, left_x, over_z, sibling, over_zl, right_y, left_y, dev(y_=yo)]
    for device in greeted:
        pl.semaphore_signal(barrier, inc=1, device_id=device, device_id_type=MESH)

    copies = Copies(send_sems, recv_sems)
    right = (right0, right1)
    chunk_width = staged.shape[3]
    pairs = (
        (ranks_hbm, ranks),
        (steps_hbm, steps),
        (slots_hbm, slots),
        (right_hbm.at[0], right[0]),
        (right_hbm.at[1], right[1]),
        (left, lefts.at[col]),
        (base.at[0], work.at[0]),
        (base.at[1], work.at[1]),
    )
    local = [pltpu.make_async_copy(src, dst, own_sems.at[n]) for n, (src, dst) in enumerate(pairs)]
    for copy in local[:6]:
        copy.start()
    for copy in local[:3]:
        copy.wait()

    ends = slot_ends(ranks, slots)
    own_rank, own_steps, all_steps = jnp.int32(0), jnp.int32(0), jnp.int32(0)
    for w in range(SLOTS):
        mine = slots[w] == col
        own_rank = own_rank + jnp.where(mine, ranks[w], 0)
        own_steps = own_steps + jnp.where(mine, steps[w], 0)
        all_steps = all_steps + steps[w]
    own_start = jnp.int32(0)
    for s in range(SLOTS - 1):
        own_start = jnp.where(col == s + 1, ends[s], own_start)

    def as_vector(v):
        return jnp.full((1, 128), v, jnp.int32).astype(F32)

    scale = ADAPTER_ALPHA * (as_vector(own_steps) / as_vector(all_steps)) / as_vector(own_rank)
    scale = jnp.concatenate([scale] * (chunk_width // 128), axis=1)

    ystar, zlstar = 2 * (x % 2) + zh, x // 2

    def a1_event(p, ystar_, zl_):
        return (p * 4 + ystar_) * 2 + zl_

    def stage(c):
        p, lo = place(c, chunk_width)
        if lo == 0:
            local[3 + p].wait()
        for t2 in range(8):
            k = jnp.bitwise_and(t2 - own_start + 64, 7)
            staged[c, t2] = (right[p][k][:, lo : lo + chunk_width].astype(F32) * scale).astype(BF16)

    def send_unit(c, n):
        dx, dz = (2, 1, 3, 0)[n % 4], n // 4
        x2, zh2 = (x + dx) % 4, (zh + dz) % 2
        src, dst = staged.at[c, x2 * 2 + zh2], first.at[c, ystar, zl]
        event, device = a1_event(c, ystar, zl), dev(x_=x2, zh_=zh2, zl_=zlstar)
        if dx == 0 and dz == 0:
            copies.start_or_local(src, dst, event, device, zl == zlstar)
        else:
            copies.start(src, dst, event, device)

    stage(0)
    pl.semaphore_wait(barrier, len(greeted))

    def send_units(c):
        if c:
            stage(c)
            copies.drain(DRAIN)
        for n in range(8):
            send_unit(c, n)

    for c in FIRST:
        send_units(c)
    for c in range(CHUNKS):
        if c not in FIRST and c in PACED.values():
            stage(c)
    L0 = N_A1 + N_A2
    own_left = lefts.at[col]
    local[5].wait()
    local[6].start()
    local[7].start()

    depth = packed_left.shape[2]
    lane = lax.broadcasted_iota(jnp.int32, (1, depth), 1)
    position = lane // 64 + 8 * ((lane // UNIT) % 4)
    lane_slot, lane_start = slot_and_start(position, ends)
    source = lane_slot * 128 + (position - lane_start) * UNIT + lane % UNIT

    def pick_left(slot, init=False):
        k = lax.broadcasted_iota(jnp.int32, (128, depth), 0) + slot * 128
        pick = jnp.where(k == source, 1.0, 0.0).astype(BF16)
        for p in range(2):
            part = jnp.dot(lefts[slot, p], pick, preferred_element_type=F32).astype(BF16)
            packed_left[p] = part if init else packed_left[p] + part

    pick_left(col, init=True)

    def a2_event(p, y_):
        return N_A1 + p * 4 + y_

    def turn(c):
        for n, dy in enumerate((2, 1, 3, 0)):
            y2 = (y + dy) % 4
            for zl0 in range(2):
                copies.arrived(first.at[c, y2, zl0], a1_event(c, y2, zl0), sibling)
            if dy:
                copies.start(first.at[c, y2], second[c].at[y], a2_event(c, y), dev(y_=y2))
            else:
                second[c][y] = first[c, y]
            if c in PACED:
                send_unit(PACED[c], 2 * n)
                send_unit(PACED[c], 2 * n + 1)

    def col_of(y_, zl_):
        return zl_ * 4 + y_

    def pass_left(base, zl_):
        c_from_left, c_from_right = col_of(yl, zl_), col_of(yr, zl_)
        copies.arrived(lefts.at[c_from_left], L0 + base, sibling)
        copies.start(lefts.at[c_from_left, 0], lefts.at[c_from_left, 0], L0 + base + 3, right_y)
        copies.arrived(lefts.at[c_from_right], L0 + base + 1, sibling)
        copies.start(lefts.at[c_from_right, 1], lefts.at[c_from_right, 1], L0 + base + 4, left_y)


    BLK = [t, xl * 2 + zh, xr * 2 + zh, xo * 2 + zh, x * 2 + zo, xl * 2 + zo, xr * 2 + zo, xo * 2 + zo]
    HALF = [pl.ds(0, 32), pl.ds(32, 32)]

    def b_event(p, n):
        return N_A1 + N_A2 + N_L + p * N_B + n

    r1 = pl.ds(0, ROUTE1_TILES * 128)
    r2 = pl.ds(ROUTE1_TILES * 128, chunk_width - ROUTE1_TILES * 128)

    def at(cols, p, blk, rows=None, half=core):
        return r.at[p, half, blk, pl.ds(0, 64) if rows is None else rows, cols]

    def go(cols, p, blk, n, device, rows=None):
        copies.start(at(cols, p, blk, rows), at(cols, p, blk, rows), b_event(p, n), device)

    def got(cols, p, blk, n, rows=None):
        copies.arrived(at(cols, p, blk, rows), b_event(p, n), sibling)

    def share(p, i):
        block = r.at[p, core, BLK[i]]
        copies.start(block, block, b_event(p, 17 + i), sibling)

    def pack(p):
        for y0 in (1, 2, 3):
            y2 = (y + y0) % 4
            copies.arrived(second[p].at[y2], a2_event(p, y2), sibling)
        for i in range(4):
            slot, _ = slot_and_start(t + 8 * i, ends)
            unit = second[p][jnp.bitwise_and(slot, 3), jnp.right_shift(slot, 2)]
            r[p, core, t, pl.ds(UNIT * i, UNIT)] = unit
        go(r2, p, t, 0, right_x)
        go(r2, p, t, 1, left_x)
        go(r1, p, t, 8, over_z)
        go(r1, p, t, 9, right_x)
        go(r1, p, t, 10, left_x)
        go(r2, p, t, 4, over_z)
        share(p, 0)

    def early(p):
        got(r2, p, BLK[1], 0)
        go(r2, p, BLK[1], 2, right_x, HALF[0])
        go(r2, p, BLK[1], 5, over_z)
        got(r2, p, BLK[2], 1)
        go(r2, p, BLK[2], 3, left_x, HALF[1])
        go(r2, p, BLK[2], 6, over_z)
        got(r1, p, BLK[4], 8)
        go(r1, p, BLK[4], 13, right_x)
        go(r1, p, BLK[4], 14, left_x)

    def middle(p):
        got(r1, p, BLK[1], 9)
        go(r1, p, BLK[1], 11, right_x, HALF[0])
        share(p, 1)
        got(r1, p, BLK[2], 10)
        go(r1, p, BLK[2], 12, left_x, HALF[1])
        share(p, 2)
        got(r2, p, BLK[3], 2, HALF[0])
        got(r2, p, BLK[3], 3, HALF[1])
        go(r2, p, BLK[3], 7, over_z)
        got(r2, p, BLK[4], 4)
        share(p, 4)

    def late(p):
        got(r1, p, BLK[5], 13)
        go(r1, p, BLK[5], 15, right_x, HALF[0])
        got(r1, p, BLK[6], 14)
        go(r1, p, BLK[6], 16, left_x, HALF[1])
        got(r1, p, BLK[3], 11, HALF[0])
        got(r1, p, BLK[3], 12, HALF[1])
        share(p, 3)
        got(r2, p, BLK[5], 5)
        share(p, 5)
        got(r2, p, BLK[6], 6)
        share(p, 6)

    def last(p):
        got(r2, p, BLK[7], 7)
        got(r1, p, BLK[7], 15, HALF[0])
        got(r1, p, BLK[7], 16, HALF[1])
        share(p, 7)

    def shared(p, blocks):
        for i in blocks:
            copies.arrived(r.at[p, co, BLK[i]], b_event(p, 17 + i), sibling)

    def start_left():
        copies.start(own_left, own_left, L0 + 0, right_y)
        copies.start(own_left, own_left, L0 + 1, left_y)

    def cross_left():
        other = lefts.at[col_of(y, zlo)]
        copies.arrived(other, L0 + 2, sibling)
        copies.start(other, other, L0 + 5, right_y)
        copies.start(other, other, L0 + 6, left_y)

    c_l, c_r, c_o, own_o = col_of(yl, zlo), col_of(yr, zlo), col_of(yo, zlo), col_of(yo, zl)

    def pass_other_left():
        copies.arrived(lefts.at[c_l], L0 + 5, sibling)
        copies.start(lefts.at[c_l, 0], lefts.at[c_l, 0], L0 + 7, right_y)
        copies.arrived(lefts.at[c_r], L0 + 6, sibling)
        copies.start(lefts.at[c_r, 1], lefts.at[c_r, 1], L0 + 8, left_y)

    def merge(c):
        for h, lo, hi in slices(chunk_width):
            merge_slice(c, h, lo, hi, work, packed_left, r)

    def own_halves():
        copies.arrived(lefts.at[own_o, 0], L0 + 3, sibling)
        copies.arrived(lefts.at[own_o, 1], L0 + 4, sibling)

    def other_halves():
        copies.arrived(lefts.at[c_o, 0], L0 + 7, sibling)
        copies.arrived(lefts.at[c_o, 1], L0 + 8, sibling)

    def load_base():
        local[6].wait()
        local[7].wait()

    steps_of = {
        "S": send_units, "T": turn, "P": pack, "E": early, "M": middle, "A": late, "Z": last, "H": lambda c: shared(c, (0, 4, 1, 2)), "I": lambda c: shared(c, (3, 5, 6)), "J": lambda c: shared(c, (7,)),
        "D": lambda n: copies.drain(10 * n), "G": merge,
        "L": lambda n: (
            start_left,
            lambda: copies.start(own_left, own_left, L0 + 2, over_zl),
            lambda: pass_left(0, zl),
            cross_left,
            pass_other_left,
            own_halves,
            other_halves,
            load_base,
        )[n](),
        "K": lambda n: pick_left(
            (col, col_of(yl, zl), col_of(yr, zl), own_o, col_of(y, zlo), c_l, c_r, c_o)[n], init=n == 0
        ),
    }
    for step in SCHEDULE:
        steps_of[step[0]](int(step[1]))
    copies.finish()


def place(chunk, width):
    per = CHUNKS // 2
    return chunk // per, (chunk % per) * width


def slices(width, step=512):
    return [(h, lo, min(lo + step, width)) for h in range(2) for lo in range(0, width, step)]


def merge_slice(c, h, lo, hi, work, packed_left, r, out=None):
    p, first = place(c, r.shape[4])
    begin = h * (work.shape[2] // 2) + first + lo
    cols = slice(begin, begin + hi - lo)
    rhs = r[c, h, :, :, lo:hi].reshape(packed_left.shape[2], hi - lo)
    delta = jnp.dot(packed_left[p], rhs, preferred_element_type=F32)
    total = (work[p, :, cols].astype(F32) + delta).astype(BF16)
    if out is None:
        work[p, :, cols] = total
    else:
        out[:, cols] = total
    return p, cols


def merge_kernel(work, packed_left, r, out, last, sems):
    width, half = r.shape[4], work.shape[2] // 2
    p, lo = place(CHUNKS - 1, width)
    pairs = [(work.at[p2], out.at[p2]) for p2 in range(p)]
    for h in range(2 if lo else 0):
        cols = slice(h * half, h * half + lo)
        pairs.append((work.at[p, :, cols], out.at[p, :, cols]))
    started = []

    def send(src, dst):
        copy = pltpu.make_async_copy(src, dst, sems.at[len(started)])
        copy.start()
        started.append(copy)

    for src, dst in pairs:
        send(src, dst)
    for h, lo, hi in slices(width):
        p, cols = merge_slice(CHUNKS - 1, h, lo, hi, work, packed_left, r, last)
        send(last.at[:, cols], out.at[p, :, cols])
    for copy in started:
        copy.wait()


def body(base, left, right, ranks, steps, slots):
    projections, rows, columns = base.shape
    half = columns // 2
    left = left.reshape(projections, rows, 128)
    right = right.reshape(projections, 8, UNIT, half)
    width = 2 * half // CHUNKS
    vmem = pl.BlockSpec(memory_space=pltpu.VMEM)
    hbm = pl.BlockSpec(memory_space=pltpu.HBM)
    r, packed_left, work = pl.pallas_call(
        gather_kernel,
        out_shape=(
            jax.ShapeDtypeStruct((CHUNKS, 2, 8, 64, width), BF16),
            jax.ShapeDtypeStruct((2, rows, 512), BF16),
            jax.ShapeDtypeStruct(base.shape, BF16),
        ),
        in_specs=[hbm] * 6,
        out_specs=(vmem,) * 3,
        scratch_shapes=[
            pltpu.SMEM((SLOTS,), jnp.int32),
            pltpu.SMEM((SLOTS,), jnp.int32),
            pltpu.SMEM((SLOTS,), jnp.int32),
            pltpu.VMEM((8, UNIT, half), BF16),
            pltpu.VMEM((8, UNIT, half), BF16),
            pltpu.VMEM((CHUNKS, 8, UNIT, width), BF16),
            pltpu.VMEM((CHUNKS, 4, 2, UNIT, width), BF16),
            *[pltpu.VMEM((4, 2, UNIT, width), BF16)] * CHUNKS,
            pltpu.VMEM((8, 2, rows, 128), BF16),
            pltpu.SemaphoreType.DMA((N_SEND,)),
            pltpu.SemaphoreType.DMA((N_RECV,)),
            pltpu.SemaphoreType.DMA((8,)),
        ],
        compiler_params=pltpu.CompilerParams(
            collective_id=0, has_side_effects=True, vmem_limit_bytes=24 * 2**20
        ),
        name="gather_factors",
    )(*[pltpu.with_memory_space_constraint(a, pltpu.HBM) for a in (ranks, steps, slots, left, right, base)])
    return pl.pallas_call(
        merge_kernel,
        out_shape=jax.ShapeDtypeStruct(base.shape, BF16),
        in_specs=[vmem] * 3,
        out_specs=pl.BlockSpec(memory_space=pltpu.HBM),
        scratch_shapes=[pltpu.VMEM((rows, columns), BF16), pltpu.SemaphoreType.DMA((16,))],
        compiler_params=pltpu.CompilerParams(vmem_limit_bytes=24 * 2**20),
        name="merge_blocks",
    )(work, packed_left, r)


def solution(mesh):
    placed = (P(None, "row", "col"), P(None, "row", "col", None), P(None, "col", None, "row"), P(), P(), P())
    return jax.shard_map(
        body, mesh=mesh, in_specs=placed, out_specs=P(None, "row", "col"), check_vma=False
    )
```

```python
import functools

import jax
import jax.numpy as jnp
from jax import lax
from jax.experimental import pallas as pl
from jax.experimental.pallas import tpu as pltpu
from jax.sharding import PartitionSpec as P

ADAPTER_ALPHA = 32
MESH = pl.DeviceIdType.MESH
BF16 = jnp.bfloat16
F32 = jnp.float32
SLOTS = 8
UNIT = 16
DRAIN = 7
CHUNKS = 2
ROUTE1_TILES = 8
FIRST = (0, 1)
PACED = {}
SCHEDULE = (
    "T0", "L1", "T1", "P0", "P1", "L0", "K0", "E0", "L3", "M0", "E1", "L2", "A0", "L4", "K1",
    "K2", "K4", "D2", "M1", "L5", "K3", "Z0", "A1", "K5", "K6", "L6", "K7", "L7", "H0", "I0",
    "J0", "G0", "D3", "H1", "D1", "Z1", "I1", "J1",
)


def slot_ends(ranks, slots):
    ends, total = [], jnp.int32(0)
    for s in range(SLOTS):
        for w in range(SLOTS):
            total = total + jnp.where(slots[w] == s, ranks[w], 0)
        ends.append(total // UNIT)
    return ends


def slot_and_start(position, ends):
    slot = jnp.zeros_like(position)
    start = jnp.zeros_like(position)
    for s in range(SLOTS - 1):
        past = position >= ends[s]
        slot = slot + jnp.where(past, 1, 0)
        start = jnp.where(past, ends[s], start)
    return slot, start


class Copies:
    def __init__(self, send_sems, recv_sems):
        self.send_sems, self.recv_sems = send_sems, recv_sems
        self.count, self.started = 0, []

    def start(self, src, dst, event, device):
        copy = pltpu.make_async_remote_copy(
            src_ref=src,
            dst_ref=dst,
            send_sem=self.send_sems.at[self.count],
            recv_sem=self.recv_sems.at[event],
            device_id=device,
            device_id_type=MESH,
        )
        self.count += 1
        copy.start()
        self.started.append((copy, None))

    def start_or_local(self, src, dst, event, device, local):
        copy = pltpu.make_async_remote_copy(
            src_ref=src,
            dst_ref=dst,
            send_sem=self.send_sems.at[self.count],
            recv_sem=self.recv_sems.at[event],
            device_id=device,
            device_id_type=MESH,
        )
        own = pltpu.make_async_copy(src, dst, self.recv_sems.at[event])
        self.count += 1
        remote = jnp.logical_not(local)
        pl.when(remote)(copy.start)
        pl.when(local)(own.start)
        self.started.append((copy, remote))

    def arrived(self, dst, event, device):
        pltpu.make_async_remote_copy(
            src_ref=dst,
            dst_ref=dst,
            send_sem=self.send_sems.at[0],
            recv_sem=self.recv_sems.at[event],
            device_id=device,
            device_id_type=MESH,
        ).wait_recv()

    def drain(self, count):
        for copy, when in self.started[:count]:
            if when is None:
                copy.wait_send()
            else:
                pl.when(when)(copy.wait_send)
        self.started = self.started[count:]

    def finish(self):
        for copy, when in self.started:
            if when is None:
                copy.wait_send()
            else:
                pl.when(when)(copy.wait_send)


N_A1, N_A2, N_L, N_B = CHUNKS * 8, CHUNKS * 4, 9, 17 + 8
N_RECV = N_A1 + N_A2 + N_L + CHUNKS * N_B
N_SEND = CHUNKS * (8 + 3 + N_B) + 9


def gather_kernel(
    ranks_hbm,
    steps_hbm,
    slots_hbm,
    left,
    right_hbm,
    base,
    r,
    packed_left,
    work,
    ranks,
    steps,
    slots,
    right0,
    right1,
    staged,
    first,
    *rest,
):
    second, (lefts, send_sems, recv_sems, own_sems) = rest[:CHUNKS], rest[CHUNKS:]
    row, col = lax.axis_index("row"), lax.axis_index("col")
    x, zh, core = row // 4, (row // 2) % 2, row % 2
    zl, y = col // 4, col % 4
    t = row // 2

    def dev(x_=x, zh_=zh, core_=core, y_=y, zl_=zl):
        return (x_ * 4 + zh_ * 2 + core_, zl_ * 4 + y_)

    xr, xl, xo = (x + 1) % 4, (x + 3) % 4, (x + 2) % 4
    yr, yl, yo = (y + 1) % 4, (y + 3) % 4, (y + 2) % 4
    zo, co, zlo = 1 - zh, 1 - core, 1 - zl
    right_x, left_x = dev(x_=xr), dev(x_=xl)
    right_y, left_y = dev(y_=yr), dev(y_=yl)
    over_z, sibling, over_zl = dev(zh_=zo), dev(core_=co), dev(zl_=zlo)

    barrier = pltpu.get_barrier_semaphore()
    greeted = []
    for a in range(2):
        for zh0 in range(2):
            for zl0 in range(2):
                greeted.append(dev(x_=2 * zl + a, zh_=zh0, zl_=zl0))
    greeted += [right_x, left_x, over_z, sibling, over_zl, right_y, left_y, dev(y_=yo)]
    for device in greeted:
        pl.semaphore_signal(barrier, inc=1, device_id=device, device_id_type=MESH)

    copies = Copies(send_sems, recv_sems)
    right = (right0, right1)
    chunk_width = staged.shape[3]
    pairs = (
        (ranks_hbm, ranks),
        (steps_hbm, steps),
        (slots_hbm, slots),
        (right_hbm.at[0], right[0]),
        (right_hbm.at[1], right[1]),
        (left, lefts.at[col]),
        (base.at[0], work.at[0]),
        (base.at[1], work.at[1]),
    )
    local = [pltpu.make_async_copy(src, dst, own_sems.at[n]) for n, (src, dst) in enumerate(pairs)]
    for copy in local[:6]:
        copy.start()
    for copy in local[:3]:
        copy.wait()

    ends = slot_ends(ranks, slots)
    own_rank, own_steps, all_steps = jnp.int32(0), jnp.int32(0), jnp.int32(0)
    for w in range(SLOTS):
        mine = slots[w] == col
        own_rank = own_rank + jnp.where(mine, ranks[w], 0)
        own_steps = own_steps + jnp.where(mine, steps[w], 0)
        all_steps = all_steps + steps[w]
    own_start = jnp.int32(0)
    for s in range(SLOTS - 1):
        own_start = jnp.where(col == s + 1, ends[s], own_start)

    def as_vector(v):
        return jnp.full((1, 128), v, jnp.int32).astype(F32)

    scale = ADAPTER_ALPHA * (as_vector(own_steps) / as_vector(all_steps)) / as_vector(own_rank)
    scale = jnp.concatenate([scale] * (chunk_width // 128), axis=1)

    ystar, zlstar = 2 * (x % 2) + zh, x // 2

    def a1_event(p, ystar_, zl_):
        return (p * 4 + ystar_) * 2 + zl_

    def stage(c):
        p, lo = place(c, chunk_width)
        if lo == 0:
            local[3 + p].wait()
        for t2 in range(8):
            k = jnp.bitwise_and(t2 - own_start + 64, 7)
            staged[c, t2] = (right[p][k][:, lo : lo + chunk_width].astype(F32) * scale).astype(BF16)

    def send_unit(c, n):
        dx, dz = (2, 1, 3, 0)[n % 4], n // 4
        x2, zh2 = (x + dx) % 4, (zh + dz) % 2
        src, dst = staged.at[c, x2 * 2 + zh2], first.at[c, ystar, zl]
        event, device = a1_event(c, ystar, zl), dev(x_=x2, zh_=zh2, zl_=zlstar)
        if dx == 0 and dz == 0:
            copies.start_or_local(src, dst, event, device, zl == zlstar)
        else:
            copies.start(src, dst, event, device)

    stage(0)
    pl.semaphore_wait(barrier, len(greeted))

    def send_units(c):
        if c:
            stage(c)
            copies.drain(DRAIN)
        for n in range(8):
            send_unit(c, n)

    for c in FIRST:
        send_units(c)
    for c in range(CHUNKS):
        if c not in FIRST and c in PACED.values():
            stage(c)
    L0 = N_A1 + N_A2
    own_left = lefts.at[col]
    local[5].wait()
    local[6].start()
    local[7].start()

    depth = packed_left.shape[2]
    lane = lax.broadcasted_iota(jnp.int32, (1, depth), 1)
    position = lane // 64 + 8 * ((lane // UNIT) % 4)
    lane_slot, lane_start = slot_and_start(position, ends)
    source = lane_slot * 128 + (position - lane_start) * UNIT + lane % UNIT

    def pick_left(slot, init=False):
        k = lax.broadcasted_iota(jnp.int32, (128, depth), 0) + slot * 128
        pick = jnp.where(k == source, 1.0, 0.0).astype(BF16)
        for p in range(2):
            part = jnp.dot(lefts[slot, p], pick, preferred_element_type=F32).astype(BF16)
            packed_left[p] = part if init else packed_left[p] + part

    pick_left(col, init=True)

    def a2_event(p, y_):
        return N_A1 + p * 4 + y_

    def turn(c):
        for n, dy in enumerate((2, 1, 3, 0)):
            y2 = (y + dy) % 4
            for zl0 in range(2):
                copies.arrived(first.at[c, y2, zl0], a1_event(c, y2, zl0), sibling)
            if dy:
                copies.start(first.at[c, y2], second[c].at[y], a2_event(c, y), dev(y_=y2))
            else:
                second[c][y] = first[c, y]
            if c in PACED:
                send_unit(PACED[c], 2 * n)
                send_unit(PACED[c], 2 * n + 1)

    def col_of(y_, zl_):
        return zl_ * 4 + y_

    def pass_left(base, zl_):
        c_from_left, c_from_right = col_of(yl, zl_), col_of(yr, zl_)
        copies.arrived(lefts.at[c_from_left], L0 + base, sibling)
        copies.start(lefts.at[c_from_left, 0], lefts.at[c_from_left, 0], L0 + base + 3, right_y)
        copies.arrived(lefts.at[c_from_right], L0 + base + 1, sibling)
        copies.start(lefts.at[c_from_right, 1], lefts.at[c_from_right, 1], L0 + base + 4, left_y)


    BLK = [t, xl * 2 + zh, xr * 2 + zh, xo * 2 + zh, x * 2 + zo, xl * 2 + zo, xr * 2 + zo, xo * 2 + zo]
    HALF = [pl.ds(0, 32), pl.ds(32, 32)]

    def b_event(p, n):
        return N_A1 + N_A2 + N_L + p * N_B + n

    r1 = pl.ds(0, ROUTE1_TILES * 128)
    r2 = pl.ds(ROUTE1_TILES * 128, chunk_width - ROUTE1_TILES * 128)

    def at(cols, p, blk, rows=None, half=core):
        return r.at[p, half, blk, pl.ds(0, 64) if rows is None else rows, cols]

    def go(cols, p, blk, n, device, rows=None):
        copies.start(at(cols, p, blk, rows), at(cols, p, blk, rows), b_event(p, n), device)

    def got(cols, p, blk, n, rows=None):
        copies.arrived(at(cols, p, blk, rows), b_event(p, n), sibling)

    def share(p, i):
        block = r.at[p, core, BLK[i]]
        copies.start(block, block, b_event(p, 17 + i), sibling)

    def pack(p):
        for y0 in (1, 2, 3):
            y2 = (y + y0) % 4
            copies.arrived(second[p].at[y2], a2_event(p, y2), sibling)
        for i in range(4):
            slot, _ = slot_and_start(t + 8 * i, ends)
            unit = second[p][jnp.bitwise_and(slot, 3), jnp.right_shift(slot, 2)]
            r[p, core, t, pl.ds(UNIT * i, UNIT)] = unit
        go(r2, p, t, 0, right_x)
        go(r2, p, t, 1, left_x)
        go(r1, p, t, 8, over_z)
        go(r1, p, t, 9, right_x)
        go(r1, p, t, 10, left_x)
        go(r2, p, t, 4, over_z)
        share(p, 0)

    def early(p):
        got(r2, p, BLK[1], 0)
        go(r2, p, BLK[1], 2, right_x, HALF[0])
        go(r2, p, BLK[1], 5, over_z)
        got(r2, p, BLK[2], 1)
        go(r2, p, BLK[2], 3, left_x, HALF[1])
        go(r2, p, BLK[2], 6, over_z)
        got(r1, p, BLK[4], 8)
        go(r1, p, BLK[4], 13, right_x)
        go(r1, p, BLK[4], 14, left_x)

    def middle(p):
        got(r1, p, BLK[1], 9)
        go(r1, p, BLK[1], 11, right_x, HALF[0])
        share(p, 1)
        got(r1, p, BLK[2], 10)
        go(r1, p, BLK[2], 12, left_x, HALF[1])
        share(p, 2)
        got(r2, p, BLK[3], 2, HALF[0])
        got(r2, p, BLK[3], 3, HALF[1])
        go(r2, p, BLK[3], 7, over_z)
        got(r2, p, BLK[4], 4)
        share(p, 4)

    def late(p):
        got(r1, p, BLK[5], 13)
        go(r1, p, BLK[5], 15, right_x, HALF[0])
        got(r1, p, BLK[6], 14)
        go(r1, p, BLK[6], 16, left_x, HALF[1])
        got(r1, p, BLK[3], 11, HALF[0])
        got(r1, p, BLK[3], 12, HALF[1])
        share(p, 3)
        got(r2, p, BLK[5], 5)
        share(p, 5)
        got(r2, p, BLK[6], 6)
        share(p, 6)

    def last(p):
        got(r2, p, BLK[7], 7)
        got(r1, p, BLK[7], 15, HALF[0])
        got(r1, p, BLK[7], 16, HALF[1])
        share(p, 7)

    def shared(p, blocks):
        for i in blocks:
            copies.arrived(r.at[p, co, BLK[i]], b_event(p, 17 + i), sibling)

    def start_left():
        copies.start(own_left, own_left, L0 + 0, right_y)
        copies.start(own_left, own_left, L0 + 1, left_y)

    def cross_left():
        other = lefts.at[col_of(y, zlo)]
        copies.arrived(other, L0 + 2, sibling)
        copies.start(other, other, L0 + 5, right_y)
        copies.start(other, other, L0 + 6, left_y)

    c_l, c_r, c_o, own_o = col_of(yl, zlo), col_of(yr, zlo), col_of(yo, zlo), col_of(yo, zl)

    def pass_other_left():
        copies.arrived(lefts.at[c_l], L0 + 5, sibling)
        copies.start(lefts.at[c_l, 0], lefts.at[c_l, 0], L0 + 7, right_y)
        copies.arrived(lefts.at[c_r], L0 + 6, sibling)
        copies.start(lefts.at[c_r, 1], lefts.at[c_r, 1], L0 + 8, left_y)

    def merge(c):
        for h, lo, hi in slices(chunk_width):
            merge_slice(c, h, lo, hi, work, packed_left, r)

    def own_halves():
        copies.arrived(lefts.at[own_o, 0], L0 + 3, sibling)
        copies.arrived(lefts.at[own_o, 1], L0 + 4, sibling)

    def other_halves():
        copies.arrived(lefts.at[c_o, 0], L0 + 7, sibling)
        copies.arrived(lefts.at[c_o, 1], L0 + 8, sibling)

    def load_base():
        local[6].wait()
        local[7].wait()

    steps_of = {
        "S": send_units, "T": turn, "P": pack, "E": early, "M": middle, "A": late, "Z": last, "H": lambda c: shared(c, (0, 4, 1, 2)), "I": lambda c: shared(c, (3, 5, 6)), "J": lambda c: shared(c, (7,)),
        "D": lambda n: copies.drain(10 * n), "G": merge,
        "L": lambda n: (
            start_left,
            lambda: copies.start(own_left, own_left, L0 + 2, over_zl),
            lambda: pass_left(0, zl),
            cross_left,
            pass_other_left,
            own_halves,
            other_halves,
            load_base,
        )[n](),
        "K": lambda n: pick_left(
            (col, col_of(yl, zl), col_of(yr, zl), own_o, col_of(y, zlo), c_l, c_r, c_o)[n], init=n == 0
        ),
    }
    for step in SCHEDULE:
        steps_of[step[0]](int(step[1]))
    copies.finish()


def place(chunk, width):
    per = CHUNKS // 2
    return chunk // per, (chunk % per) * width


def slices(width, step=512):
    return [(h, lo, min(lo + step, width)) for h in range(2) for lo in range(0, width, step)]


def merge_slice(c, h, lo, hi, work, packed_left, r, out=None):
    p, first = place(c, r.shape[4])
    begin = h * (work.shape[2] // 2) + first + lo
    cols = slice(begin, begin + hi - lo)
    rhs = r[c, h, :, :, lo:hi].reshape(packed_left.shape[2], hi - lo)
    delta = jnp.dot(packed_left[p], rhs, preferred_element_type=F32)
    total = (work[p, :, cols].astype(F32) + delta).astype(BF16)
    if out is None:
        work[p, :, cols] = total
    else:
        out[:, cols] = total
    return p, cols


def merge_kernel(work, packed_left, r, out, last, sems):
    width, half = r.shape[4], work.shape[2] // 2
    p, lo = place(CHUNKS - 1, width)
    pairs = [(work.at[p2], out.at[p2]) for p2 in range(p)]
    for h in range(2 if lo else 0):
        cols = slice(h * half, h * half + lo)
        pairs.append((work.at[p, :, cols], out.at[p, :, cols]))
    started = []

    def send(src, dst):
        copy = pltpu.make_async_copy(src, dst, sems.at[len(started)])
        copy.start()
        started.append(copy)

    for src, dst in pairs:
        send(src, dst)
    for h, lo, hi in slices(width):
        p, cols = merge_slice(CHUNKS - 1, h, lo, hi, work, packed_left, r, last)
        send(last.at[:, cols], out.at[p, :, cols])
    for copy in started:
        copy.wait()


def body(base, left, right, ranks, steps, slots):
    projections, rows, columns = base.shape
    half = columns // 2
    left = left.reshape(projections, rows, 128)
    right = right.reshape(projections, 8, UNIT, half)
    width = 2 * half // CHUNKS
    vmem = pl.BlockSpec(memory_space=pltpu.VMEM)
    hbm = pl.BlockSpec(memory_space=pltpu.HBM)
    r, packed_left, work = pl.pallas_call(
        gather_kernel,
        out_shape=(
            jax.ShapeDtypeStruct((CHUNKS, 2, 8, 64, width), BF16),
            jax.ShapeDtypeStruct((2, rows, 512), BF16),
            jax.ShapeDtypeStruct(base.shape, BF16),
        ),
        in_specs=[hbm] * 6,
        out_specs=(vmem,) * 3,
        scratch_shapes=[
            pltpu.SMEM((SLOTS,), jnp.int32),
            pltpu.SMEM((SLOTS,), jnp.int32),
            pltpu.SMEM((SLOTS,), jnp.int32),
            pltpu.VMEM((8, UNIT, half), BF16),
            pltpu.VMEM((8, UNIT, half), BF16),
            pltpu.VMEM((CHUNKS, 8, UNIT, width), BF16),
            pltpu.VMEM((CHUNKS, 4, 2, UNIT, width), BF16),
            *[pltpu.VMEM((4, 2, UNIT, width), BF16)] * CHUNKS,
            pltpu.VMEM((8, 2, rows, 128), BF16),
            pltpu.SemaphoreType.DMA((N_SEND,)),
            pltpu.SemaphoreType.DMA((N_RECV,)),
            pltpu.SemaphoreType.DMA((8,)),
        ],
        compiler_params=pltpu.CompilerParams(
            collective_id=0, has_side_effects=True, vmem_limit_bytes=24 * 2**20
        ),
        name="gather_factors",
    )(*[pltpu.with_memory_space_constraint(a, pltpu.HBM) for a in (ranks, steps, slots, left, right, base)])
    return pl.pallas_call(
        merge_kernel,
        out_shape=jax.ShapeDtypeStruct(base.shape, BF16),
        in_specs=[vmem] * 3,
        out_specs=pl.BlockSpec(memory_space=pltpu.HBM),
        scratch_shapes=[pltpu.VMEM((rows, columns), BF16), pltpu.SemaphoreType.DMA((16,))],
        compiler_params=pltpu.CompilerParams(vmem_limit_bytes=24 * 2**20),
        name="merge_blocks",
    )(work, packed_left, r)


def solution(mesh):
    placed = (P(None, "row", "col"), P(None, "row", "col", None), P(None, "col", None, "row"), P(), P(), P())
    return jax.shard_map(
        body, mesh=mesh, in_specs=placed, out_specs=P(None, "row", "col"), check_vma=False
    )
```
